128 devices in a mesh: sec: 32 (over y, x_hi, z), tile: 4 (over x_lo, core).
Axes of the slice: x: 4 (x_hi: 2, x_lo: 2; x = x_hi * 2 + x_lo), y: 4, z: 4, core: 2. Of those that a mesh axis runs over, the one named last changes fastest.
Arguments:
- images: bfloat16 [64, 128, 256], P('sec', 'tile'), may hold values from -6 to 6
- seam_links: int32 [64, 3], replicated, may hold values 0 or 1
- partners: int32 [64, 3], P('sec'), may hold values from 0 to 63, as said below
- enc_first: bfloat16 [64, 1, 3, 3], replicated, may hold values from -3 to 3
- enc_second: bfloat16 [64, 64, 3, 3], replicated, may hold values from -0.375 to 0.375
- enc_third: bfloat16 [32, 64, 1, 1], replicated, may hold values from -1 to 1
- dec_first: bfloat16 [64, 81, 3, 3], replicated, may hold values from -0.3125 to 0.3125
- dec_second: bfloat16 [64, 64, 3, 3], replicated, may hold values from -0.375 to 0.375
- dec_third: bfloat16 [2, 64, 3, 3], replicated, may hold values from -0.375 to 0.375
Outputs:
- descriptors: bfloat16 [64, 32, 64, 128], P('sec', None, 'tile')
- flows: float32 [64, 3, 2, 64, 128], P('sec', None, None, 'tile')
The draws below stay inside these ranges and needn't reach their ends.
Inputs may be any that keep to these rules, and one draw needn't show every extreme that they name: partners[s, j] is s + o or s - o, with o = 1, 2, 4 for j = 0, 1, 2.
All inputs are finite; a program needn't handle non-finite values.
Results may differ from the reference program's by a relative error of at most 0.0098.
Values may be sent and summed in bfloat16 or wider, within the bound.
A program may use at most 128 MiB of HBM per device.

```python
import math
import jax
import jax.numpy as jnp
from jax import lax

TILE_H = 32
TILE_W = 256
ENC_CH = 64
DESC = 32
DEC_CH = 64
RADIUS = 4
DISP = 81
SECTIONS = 64
IMG_H = 128
N_TILE = 4


def draw_partners(key, part):
    section_ids = jnp.arange(SECTIONS, dtype=jnp.int32)
    columns = []
    for slot_index, offset in enumerate((1, 2, 4)):
        coin_flips = jax.random.randint(jax.random.fold_in(key, 17 + slot_index), (SECTIONS,), 0, 2)
        forward_flag = jnp.where(section_ids == SECTIONS - 1 - offset, 1, jnp.where(section_ids == offset, 0, coin_flips))
        forward_flag = jnp.where(section_ids < offset, 1, jnp.where(section_ids >= SECTIONS - offset, 0, forward_flag))
        columns.append(jnp.where(forward_flag == 1, section_ids + offset, section_ids - offset))
    return jnp.stack(columns, axis=1).astype(jnp.int32)


def set_ends(entries, own_key, low, largest):
    longest = entries.shape.index(max(entries.shape))
    spots = []
    for shift in (0, 1):
        where = [jax.random.randint(jax.random.fold_in(own_key, axis), (), 0, length) for axis, length in enumerate(entries.shape)]
        where[longest] = (where[longest] + shift) % entries.shape[longest]
        spots.append(tuple(where))
    return entries.at[spots[0]].set(low).at[spots[1]].set(largest)


def shard_levels(key, extent, shards, least, high):
    loudness, own = 1.0, jax.random.fold_in(key, 6)
    for dim, parts in shards:
        draws = jnp.exp(jax.random.uniform(jax.random.fold_in(own, dim), (parts,), jnp.float32, least / len(shards), high / len(shards)))
        loudness = loudness * jnp.repeat(draws, extent[dim] // parts).reshape([-1 if axis == dim else 1 for axis in range(len(extent))])
    return loudness


def centred(key, dims, scale, bound, cuts=(), kind=jnp.bfloat16):
    gain = shard_levels(key, dims, cuts, -0.22, 0.18) if cuts else 1.0
    values = jax.random.normal(key, dims, jnp.float32) * scale * gain
    return jnp.minimum(jnp.maximum(values, -bound), bound).astype(kind)


def setup_inputs(seed: int = 0) -> dict:
    streams_of = jax.random.split(jax.random.key(seed), 10)
    images = centred(streams_of[0], (SECTIONS, IMG_H, TILE_W), 1.0, 6.0, ((0, 32), (1, 4)))
    seam_links = set_ends((jax.random.randint(streams_of[1], (SECTIONS, N_TILE - 1), 0, 8) < 7).astype(jnp.int32), jax.random.fold_in(streams_of[1], 1), 0, 1)
    partners = draw_partners(jax.random.fold_in(streams_of[9], 71), 0)
    enc_first = centred(streams_of[3], (ENC_CH, 1, 3, 3), 4 ** -0.5, 3.0)
    enc_second = centred(streams_of[4], (ENC_CH, ENC_CH, 3, 3), (ENC_CH * 9 // 2) ** -0.5, 0.375)
    enc_third = centred(streams_of[5], (DESC, ENC_CH, 1, 1), (ENC_CH // 2) ** -0.5, 1.0)
    dec_first = centred(streams_of[6], (DEC_CH, DISP, 3, 3), (DISP * 9 // 2) ** -0.5, 0.3125)
    dec_second = centred(streams_of[7], (DEC_CH, DEC_CH, 3, 3), (DEC_CH * 9 // 2) ** -0.5, 0.375)
    dec_third = centred(streams_of[8], (2, DEC_CH, 3, 3), (DEC_CH * 9 // 2) ** -0.5, 0.375)
    return {"images": images, "seam_links": seam_links, "partners": partners, "enc_first": enc_first, "enc_second": enc_second, "enc_third": enc_third, "dec_first": dec_first, "dec_second": dec_second, "dec_third": dec_third}


leak_slope = 0.1

def leaky_relu(values):
    return jnp.maximum(values, leak_slope * values)

def convolve(values, kernel, stride, dilation):
    width_pad = dilation * (kernel.shape[3] // 2)
    return lax.conv_general_dilated(values.astype(jnp.float32), kernel.astype(jnp.float32), (stride, stride), ((0, 0), (width_pad, width_pad)), rhs_dilation=(dilation, dilation), dimension_numbers=('NCHW', 'OIHW', 'NCHW'), precision=lax.Precision.HIGHEST)

def link_pair(links_row):
    linked = links_row.astype(jnp.float32)
    nothing = jnp.zeros((1,), jnp.float32)
    return (jnp.concatenate([nothing, linked]), jnp.concatenate([linked, nothing]))

def extend(values, margin, lower_link, upper_link):
    blank_rows = jnp.zeros_like(values[:1, ..., :margin, :])
    below_rows = jnp.concatenate([blank_rows, values[:-1, ..., values.shape[-2] - margin:, :]], axis=0)
    above_rows = jnp.concatenate([values[1:, ..., :margin, :], blank_rows], axis=0)
    target_shape = (-1,) + (1,) * (values.ndim - 1)
    below_rows = below_rows * lower_link.reshape(target_shape).astype(values.dtype)
    above_rows = above_rows * upper_link.reshape(target_shape).astype(values.dtype)
    return jnp.concatenate([below_rows, values, above_rows], axis=-2)

def encode(section_image, links_row, encoder_weights):
    first_kernel, second_kernel, third_kernel = encoder_weights
    lower_link, upper_link = link_pair(links_row)
    tile_rows = section_image.reshape(N_TILE, TILE_H, TILE_W)
    blank_rows = jnp.zeros_like(tile_rows[:1, -1:, :])
    edge_rows = jnp.concatenate([blank_rows, tile_rows[:-1, -1:, :]], axis=0)
    edge_rows = edge_rows * lower_link[:, None, None].astype(tile_rows.dtype)
    stacked = jnp.concatenate([edge_rows, tile_rows], axis=1)[:, None]
    first_maps = leaky_relu(convolve(stacked, first_kernel, 2, 1)).astype(jnp.bfloat16)
    widened = extend(first_maps, 2, lower_link, upper_link)
    second_maps = leaky_relu(convolve(widened, second_kernel, 1, 2)).astype(jnp.bfloat16)
    return convolve(second_maps, third_kernel, 1, 1).astype(jnp.bfloat16)

def correlate(own_desc, partner_desc):
    window_span = 2 * RADIUS + 1
    height = own_desc.shape[2]
    breadth = own_desc.shape[3]
    padded_rows = jnp.pad(partner_desc, ((0, 0), (0, 0), (0, 0), (RADIUS, RADIUS)))
    own_wide = own_desc.astype(jnp.float32)
    terms = [lax.optimization_barrier(jnp.sum(own_wide * padded_rows[:, :, row_shift:row_shift + height, col_shift:col_shift + breadth].astype(jnp.float32), axis=1)) for row_shift in range(window_span) for col_shift in range(window_span)]
    return (jnp.stack(terms, axis=1) / math.sqrt(DESC)).astype(jnp.bfloat16)

def decode(cost_volume, lower_link, upper_link, decoder_weights):
    hidden = cost_volume
    for layer_index, kernel in enumerate(decoder_weights):
        result = convolve(extend(hidden, 1, lower_link, upper_link), kernel, 1, 1)
        if layer_index < len(decoder_weights) - 1:
            hidden = leaky_relu(result).astype(jnp.bfloat16)
        else:
            hidden = result
    return hidden

def reference(images, seam_links, partners, enc_first, enc_second, enc_third, dec_first, dec_second, dec_third):
    encoder_weights = (enc_first, enc_second, enc_third)
    decoder_weights = (dec_first, dec_second, dec_third)

    def encode_section(inputs):
        return encode(inputs[0], inputs[1], encoder_weights)
    all_desc = lax.map(encode_section, (images, seam_links))

    def decode_section(section):
        own_desc = all_desc[section]
        lower_link, upper_link = link_pair(seam_links[section])
        flow_list = []
        for slot_index in range(3):
            target = partners[section, slot_index]
            partner_lower, partner_upper = link_pair(seam_links[target])
            partner_desc = extend(all_desc[target], RADIUS, partner_lower, partner_upper)
            cost_volume = correlate(own_desc, partner_desc)
            flow_list.append(decode(cost_volume, lower_link, upper_link, decoder_weights))
        return jnp.stack(flow_list)
    flows = lax.map(decode_section, jnp.arange(SECTIONS, dtype=jnp.int32))
    descriptors = all_desc.transpose(0, 2, 1, 3, 4).reshape(SECTIONS, DESC, IMG_H // 2, TILE_W // 2)
    flows = flows.transpose(0, 1, 3, 2, 4, 5).reshape(SECTIONS, 3, 2, IMG_H // 2, TILE_W // 2)
    return (descriptors, flows)
```

```python
import functools
import math

import jax
import jax.numpy as jnp
from jax import lax
from jax.experimental import pallas as pl
from jax.experimental.pallas import tpu as pltpu
from jax.sharding import PartitionSpec as P

MESH = pl.DeviceIdType.MESH
F32, BF16 = jnp.float32, jnp.bfloat16

RADIUS = 4
SPAN = 2 * RADIUS + 1
DISP = SPAN * SPAN
OFFSETS = (1, 2, 4)
ROWS = 16
COLS = 128
CH = 64
DESC = 32
K1 = 248
EXT = ROWS + 2 * RADIUS


def leaky(v):
    return jnp.maximum(v, 0.1 * v)


def dot(a, b):
    return jnp.dot(a, b, preferred_element_type=F32)


def fold(out, half, shift, rows):
    lane = lax.broadcasted_iota(jnp.int32, (rows, COLS), 1)
    cols = slice(half * COLS, (half + 1) * COLS)
    left = pltpu.roll(out[0:rows, cols], shift, 1)
    right = pltpu.roll(out[2 * rows : 3 * rows, cols], COLS - shift, 1)
    return (
        jnp.where(lane >= shift, left, 0.0)
        + out[rows : 2 * rows, cols]
        + jnp.where(lane < COLS - shift, right, 0.0)
    )


def kernel(
    n_sec, n_tile, seam, partners, img, w1, w2, w3, d1, d2, d3, desc_out, flow_out,
    img_lo, img_hi, taps, pick, w1m, w2m, w3m, d1m, d2m, d3m, first3, desc_cy, own_rot, held, part,
    cost3, edge_out, edge_in, hid1, hid2, flow_y,
    img_send, img_recv, sec_send, sec_recv, rim_send, rim_recv, edge_send, edge_recv,
):
    sec, tile = lax.axis_index("sec"), lax.axis_index("tile")

    def at(k, dt):
        return (lax.rem(sec + k + n_sec, n_sec), lax.rem(tile + dt + n_tile, n_tile))

    peers = [(k, dt) for k in (0, -1, 1, -2, 2) for dt in (-1, 0, 1) if (k, dt) != (0, 0)]
    barrier = pltpu.get_barrier_semaphore()
    for k, dt in peers:
        pl.semaphore_signal(barrier, inc=1, device_id=at(k, dt), device_id_type=MESH)

    row_i = lax.broadcasted_iota(jnp.int32, (2 * COLS, COLS), 0)
    col_i = lax.broadcasted_iota(jnp.int32, (2 * COLS, COLS), 1)
    for kx in range(3):
        pick[:, kx * COLS : (kx + 1) * COLS] = jnp.where(row_i == 2 * col_i + (kx - 1), 1.0, 0.0).astype(BF16)
    taps[...] = jnp.zeros_like(taps)
    w1f = w1[...].astype(F32)
    for ky in range(3):
        taps[3 * ky : 3 * ky + 3, 0:CH] = w1f[ky]
    w1m[...] = taps[0:COLS, :].T[0:CH, 0:16].astype(BF16)
    w3m[...] = w3[...]
    for kx in range(3):
        rows = slice(kx * CH, (kx + 1) * CH)
        w2m[rows, :] = jnp.concatenate([w2[ky, kx].astype(F32) for ky in range(3)], axis=1).astype(BF16)
        d2m[rows, :] = jnp.concatenate([d2[ky, kx].astype(F32) for ky in range(3)], axis=1).astype(BF16)
        d1m[rows, :] = jnp.concatenate(
            [d1[ky, kx].astype(F32) for ky in range(3)] + [jnp.zeros((CH, K1 - 3 * DISP), F32)], axis=1
        ).astype(BF16)
    d3m[...] = jnp.zeros_like(d3m)
    for kx in range(3):
        d3m[kx * 8 : kx * 8 + 2, :] = jnp.concatenate([d3[ky, kx].astype(F32) for ky in range(3)], axis=1)
    for n in range(6):
        for y in range(ROWS + 2):
            cost3[n, y * K1 + 240 : y * K1 + K1, :] = jnp.zeros((8, COLS), F32)

    def link(section, side):
        place = tile - 1 + side
        inside = jnp.logical_and(place >= 0, place < n_tile - 1)
        place = jnp.clip(place, 0, n_tile - 2)
        section = jnp.clip(section, 0, 2 * n_sec - 1)
        return jnp.where(inside, seam[place, section], 0).astype(F32)

    pl.semaphore_wait(barrier, len(peers))

    def img_copy(direction):
        if direction == 0:
            src, dst, dt = img.at[:, 16:32, :], img_lo, 1
        else:
            src, dst, dt = img.at[:, 0:16, :], img_hi, -1
        return pltpu.make_async_remote_copy(
            src_ref=src, dst_ref=dst, send_sem=img_send.at[direction], recv_sem=img_recv.at[direction],
            device_id=at(0, dt), device_id_type=MESH,
        )

    for direction in (0, 1):
        img_copy(direction).start()
    for direction in (0, 1):
        img_copy(direction).wait()

    base = 2 * sec

    def encode(s, carry):
        lower, upper = link(base + s, 0), link(base + s, 1)
        below = dot(img_lo[s], pick[...]) * lower
        mid = dot(img[s], pick[...])
        above = dot(img_hi[s], pick[...]) * upper
        for kx in range(3):
            cols = slice(kx * COLS, (kx + 1) * COLS)
            taps[pl.ds(kx, 16, stride=3), :] = below[:, cols]
            taps[pl.ds(48 + kx, 32, stride=3), :] = mid[:, cols]
            taps[pl.ds(144 + kx, 16, stride=3), :] = above[:, cols]

        def first(p, carry):
            x = jnp.concatenate([taps[pl.ds(12 * p + 33, 16), :], taps[pl.ds(12 * p + 39, 16), :]], axis=1)
            v = leaky(dot(w1m[...], x.astype(BF16))) * jnp.where(p == 9, upper, 1.0)
            v = v.astype(BF16)
            for h in range(2):
                vh = v[:, h * COLS : (h + 1) * COLS]
                first3[2 * p + h + 4, 0:CH, :] = vh
                first3[2 * p + h + 2, CH : 2 * CH, :] = vh
                first3[2 * p + h, 2 * CH : 3 * CH, :] = vh
            return carry

        lax.fori_loop(0, 10, first, 0)

        def second(q, carry):
            x = jnp.concatenate([first3[2 * q + 4], first3[2 * q + 5]], axis=1)
            o = dot(w2m[...], x)
            z = jnp.concatenate([leaky(fold(o, h, 2, CH)).astype(BF16) for h in range(2)], axis=1)
            d = dot(w3m[...], z).astype(BF16)
            for h in range(2):
                dh = d[:, h * COLS : (h + 1) * COLS]
                held[4 + s, RADIUS + 2 * q + h] = dh
                desc_cy[s, pl.ds(2 * q + h, DESC, stride=ROWS), :] = dh.astype(F32)
            return carry

        lax.fori_loop(0, ROWS // 2, second, 0)
        return carry

    lax.fori_loop(0, 2, encode, 0)

    def sec_copy(k, i):
        return pltpu.make_async_remote_copy(
            src_ref=held.at[4:6, RADIUS : RADIUS + ROWS],
            dst_ref=held.at[4 - 2 * k : 6 - 2 * k, RADIUS : RADIUS + ROWS],
            send_sem=sec_send.at[i], recv_sem=sec_recv.at[i],
            device_id=at(k, 0), device_id_type=MESH,
        )

    def rim_copy(k, dt, i):
        if dt < 0:
            src, dst = slice(RADIUS, 2 * RADIUS), slice(RADIUS + ROWS, EXT)
        else:
            src, dst = slice(ROWS, RADIUS + ROWS), slice(0, RADIUS)
        return pltpu.make_async_remote_copy(
            src_ref=held.at[4:6, src],
            dst_ref=held.at[4 - 2 * k : 6 - 2 * k, dst],
            send_sem=rim_send.at[i], recv_sem=rim_recv.at[i],
            device_id=at(k, dt), device_id_type=MESH,
        )

    near = [sec_copy(-1, 0), sec_copy(1, 1)]
    near += [rim_copy(k, dt, 2 * i + (dt > 0)) for i, k in enumerate((0, -1, 1)) for dt in (-1, 1)]
    far = [sec_copy(-2, 2), sec_copy(2, 3)]
    far += [rim_copy(k, dt, 6 + 2 * i + (dt > 0)) for i, k in enumerate((-2, 2)) for dt in (-1, 1)]
    for copy in near + far:
        copy.start()

    lane = lax.broadcasted_iota(jnp.int32, (COLS, COLS), 1)

    def spread(i, carry):
        s, chunk = i // 4, lax.rem(i, 4)
        rows = pl.ds(pl.multiple_of(chunk * COLS, COLS), COLS)
        own = desc_cy[s, rows, :]
        desc_out[s, pl.ds(chunk * 8, 8)] = own.reshape(8, ROWS, COLS).astype(BF16)
        scaled = own * (1.0 / math.sqrt(DESC))
        for b in range(SPAN):
            d = b - RADIUS
            moved = pltpu.roll(scaled, d % COLS, 1) if d else scaled
            keep = jnp.logical_and(lane - d >= 0, lane - d < COLS)
            own_rot[s, b, rows, :] = jnp.where(keep, moved, 0.0)
        return carry

    lax.fori_loop(0, 8, spread, 0)

    def edge_copy(stage, n, direction):
        if stage == 0:
            src, dst = edge_out.at[n, direction], edge_in.at[n, direction]
        else:
            buf = (hid1, hid2)[stage - 1]
            if direction == 0:
                src, dst = buf.at[n, 1, CH : 2 * CH], buf.at[n, ROWS, 2 * CH : 3 * CH]
            else:
                src, dst = buf.at[n, ROWS, CH : 2 * CH], buf.at[n, 1, 0:CH]
        return pltpu.make_async_remote_copy(
            src_ref=src, dst_ref=dst,
            send_sem=edge_send.at[stage, n, direction], recv_sem=edge_recv.at[stage, n, direction],
            device_id=at(0, 2 * direction - 1), device_id_type=MESH,
        )

    def correlate(j, s):
        n = 2 * j + s
        offset = OFFSETS[j]
        own_id = base + s
        flag = partners[s, j] == own_id + offset
        lower = jnp.where(flag, link(own_id + offset, 0), link(own_id - offset, 0))
        upper = jnp.where(flag, link(own_id + offset, 1), link(own_id - offset, 1))

        def gather(y, carry):
            ahead = held[4 + s + offset, y].astype(F32)
            behind = held[4 + s - offset, y].astype(F32)
            m = jnp.where(y < RADIUS, lower, jnp.where(y >= RADIUS + ROWS, upper, 1.0))
            part[pl.ds(y, DESC, stride=EXT), :] = jnp.where(flag, ahead, behind) * m
            return carry

        lax.fori_loop(0, EXT, gather, 0)

        def column(b, carry):
            def channel(c, acc):
                own = own_rot[s, b, pl.ds(pl.multiple_of(c * ROWS, ROWS), ROWS), :]
                start = pl.multiple_of(c * EXT, 8)
                return tuple(acc[a] + own * part[pl.ds(start + a, ROWS), :] for a in range(SPAN))

            acc = lax.fori_loop(
                0, DESC, channel, tuple(jnp.zeros((ROWS, COLS), F32) for _ in range(SPAN)), unroll=4
            )
            shift = lax.rem(COLS + RADIUS - b, COLS)
            for a in range(SPAN):
                moved = pltpu.roll(acc[a], shift, 1)
                d = a * SPAN + b
                for ky in range(3):
                    cost3[n, pl.ds((2 - ky) * K1 + ky * DISP + d, ROWS, stride=K1), :] = moved
            return carry

        lax.fori_loop(0, SPAN, column, 0)
        edge_out[n, 0] = cost3[n, K1 + DISP : K1 + DISP + 88, :]
        edge_out[n, 1] = cost3[n, ROWS * K1 + DISP : ROWS * K1 + DISP + 88, :]
        for direction in (0, 1):
            edge_copy(0, n, direction).start()

    for j in range(3):
        if j == 0:
            for copy in near:
                copy.wait_recv()
        if j == 2:
            for copy in far:
                copy.wait_recv()

        def one(s, carry, j=j):
            correlate(j, s)
            return carry

        lax.fori_loop(0, 2, one, 0)

    def hidden_rows(n, q, o, buf):
        for h in range(2):
            v = leaky(fold(o, h, 1, CH)).astype(BF16)
            for ky in range(3):
                buf[n, 2 * q + h + 2 - ky, ky * CH : (ky + 1) * CH, :] = v

    def decode_one(n, carry):
        s = lax.rem(n, 2)
        for direction in (0, 1):
            edge_copy(0, n, direction).wait_recv()
        cost3[n, K1 : K1 + DISP, :] = edge_in[n, 1, 0:DISP, :] * link(base + s, 0)
        cost3[n, ROWS * K1 + 2 * DISP : ROWS * K1 + 3 * DISP, :] = edge_in[n, 0, 0:DISP, :] * link(base + s, 1)

        def rows(q, carry):
            start = pl.multiple_of((2 * q + 1) * K1, 8)
            x = jnp.concatenate([cost3[n, pl.ds(start, K1), :], cost3[n, pl.ds(start + K1, K1), :]], axis=1)
            hidden_rows(n, q, dot(d1m[...], x.astype(BF16)), hid1)
            return carry

        lax.fori_loop(0, ROWS // 2, rows, 0)
        for direction in (0, 1):
            edge_copy(1, n, direction).start()
        return carry

    lax.fori_loop(0, 6, decode_one, 0)

    def rims(stage, n, buf):
        s = lax.rem(n, 2)
        for direction in (0, 1):
            edge_copy(stage, n, direction).wait_recv()
        buf[n, 1, 0:CH, :] = (buf[n, 1, 0:CH, :].astype(F32) * link(base + s, 0)).astype(BF16)
        top = slice(2 * CH, 3 * CH)
        buf[n, ROWS, top, :] = (buf[n, ROWS, top, :].astype(F32) * link(base + s, 1)).astype(BF16)

    def decode_two(n, carry):
        rims(1, n, hid1)

        def rows(q, carry):
            x = jnp.concatenate([hid1[n, 2 * q + 1], hid1[n, 2 * q + 2]], axis=1)
            hidden_rows(n, q, dot(d2m[...], x), hid2)
            return carry

        lax.fori_loop(0, ROWS // 2, rows, 0)
        for direction in (0, 1):
            edge_copy(2, n, direction).start()
        return carry

    lax.fori_loop(0, 6, decode_two, 0)

    def decode_three(n, carry):
        rims(2, n, hid2)
        weights = d3m[...].astype(BF16)

        def rows(q, carry):
            x = jnp.concatenate([hid2[n, 2 * q + 1], hid2[n, 2 * q + 2]], axis=1)
            o = dot(weights, x)
            for h in range(2):
                flow_y[pl.ds(pl.multiple_of((2 * q + h) * 8, 8), 8), :] = fold(o, h, 1, 8)
            return carry

        lax.fori_loop(0, ROWS // 2, rows, 0)
        s, j = lax.rem(n, 2), n // 2
        for o in range(2):
            flow_out[s, j, o] = flow_y[pl.ds(o, ROWS, stride=8), :]
        return carry

    lax.fori_loop(0, 6, decode_three, 0)

    for direction in (0, 1):
        pass
    for copy in near + far:
        copy.wait_send()

    def drain(n, carry):
        for stage in range(3):
            for direction in (0, 1):
                edge_copy(stage, n, direction).wait_send()
        return carry

    lax.fori_loop(0, 6, drain, 0)


def solution(mesh):
    n_sec, n_tile = mesh.shape["sec"], mesh.shape["tile"]
    vmem = pl.BlockSpec(memory_space=pltpu.VMEM)
    smem = pl.BlockSpec(memory_space=pltpu.SMEM)
    dma = pltpu.SemaphoreType.DMA

    def shards(images, seam_links, partners, enc_first, enc_second, enc_third, dec_first, dec_second, dec_third):
        taps_first = lambda w: jnp.transpose(w, (2, 3, 0, 1))
        return pl.pallas_call(
            functools.partial(kernel, n_sec, n_tile),
            out_shape=(
                jax.ShapeDtypeStruct((2, DESC, ROWS, COLS), BF16),
                jax.ShapeDtypeStruct((2, 3, 2, ROWS, COLS), F32),
            ),
            in_specs=[smem, smem] + [vmem] * 7,
            out_specs=(vmem, vmem),
            scratch_shapes=[
                pltpu.VMEM((2, 16, 256), BF16),
                pltpu.VMEM((2, 16, 256), BF16),
                pltpu.VMEM((192, COLS), F32),
                pltpu.VMEM((256, 3 * COLS), BF16),
                pltpu.VMEM((CH, 16), BF16),
                pltpu.VMEM((3 * CH, 3 * CH), BF16),
                pltpu.VMEM((DESC, CH), BF16),
                pltpu.VMEM((3 * CH, K1), BF16),
                pltpu.VMEM((3 * CH, 3 * CH), BF16),
                pltpu.VMEM((24, 3 * CH), F32),
                pltpu.VMEM((24, 3 * CH, COLS), BF16),
                pltpu.VMEM((2, DESC * ROWS, COLS), F32),
                pltpu.VMEM((2, SPAN, DESC * ROWS, COLS), F32),
                pltpu.VMEM((10, EXT, DESC, COLS), BF16),
                pltpu.VMEM((DESC * EXT, COLS), F32),
                pltpu.VMEM((6, (ROWS + 2) * K1, COLS), F32),
                pltpu.VMEM((6, 2, 88, COLS), F32),
                pltpu.VMEM((6, 2, 88, COLS), F32),
                pltpu.VMEM((6, ROWS + 2, 3 * CH, COLS), BF16),
                pltpu.VMEM((6, ROWS + 2, 3 * CH, COLS), BF16),
                pltpu.VMEM((ROWS * 8, COLS), F32),
                dma((2,)), dma((2,)), dma((4,)), dma((4,)), dma((10,)), dma((10,)),
                dma((3, 6, 2)), dma((3, 6, 2)),
            ],
            compiler_params=pltpu.CompilerParams(
                collective_id=0, has_side_effects=True, vmem_limit_bytes=56 * 1024 * 1024
            ),
        )(
            jnp.transpose(seam_links), partners, images,
            jnp.transpose(enc_first, (1, 2, 3, 0))[0], taps_first(enc_second), taps_first(enc_third)[0, 0],
            taps_first(dec_first), taps_first(dec_second), taps_first(dec_third),
        )

    return jax.shard_map(
        shards,
        mesh=mesh,
        in_specs=(P("sec", "tile", None), P(), P("sec", None), P(), P(), P(), P(), P(), P()),
        out_specs=(P("sec", None, "tile", None), P("sec", None, None, "tile", None)),
        check_vma=False,
    )
```

```python
import functools
import math

import jax
import jax.numpy as jnp
from jax import lax
from jax.experimental import pallas as pl
from jax.experimental.pallas import tpu as pltpu
from jax.sharding import PartitionSpec as P

MESH = pl.DeviceIdType.MESH
F32, BF16 = jnp.float32, jnp.bfloat16

RADIUS = 4
SPAN = 2 * RADIUS + 1
DISP = SPAN * SPAN
OFFSETS = (1, 2, 4)
ROWS = 16
COLS = 128
CH = 64
DESC = 32
K1 = 248
EXT = ROWS + 2 * RADIUS


def leaky(v):
    return jnp.maximum(v, 0.1 * v)


def dot(a, b):
    return jnp.dot(a, b, preferred_element_type=F32)


def fold(out, half, shift, rows):
    lane = lax.broadcasted_iota(jnp.int32, (rows, COLS), 1)
    cols = slice(half * COLS, (half + 1) * COLS)
    left = pltpu.roll(out[0:rows, cols], shift, 1)
    right = pltpu.roll(out[2 * rows : 3 * rows, cols], COLS - shift, 1)
    return (
        jnp.where(lane >= shift, left, 0.0)
        + out[rows : 2 * rows, cols]
        + jnp.where(lane < COLS - shift, right, 0.0)
    )


def kernel(
    n_sec, n_tile, seam, partners, img, w1, w2, w3, d1, d2, d3, desc_out, flow_out,
    own_img, far_img, taps, pick, w1m, w2m, w3m, d1m, d2m, d3m, first3, desc_cy, own_rot, held, part, far_part,
    cost3, edge_out, edge_in, hid1, hid2, flow_y,
    img_send, img_recv, near_send, near_recv, edge_send, edge_recv,
):
    sec, tile = lax.axis_index("sec"), lax.axis_index("tile")

    def at(k, dt):
        return (lax.rem(sec + k + n_sec, n_sec), lax.rem(tile + dt + n_tile, n_tile))

    peers = [(k, dt) for k in (0, -1, 1, -2, 2) for dt in (-1, 0, 1) if (k, dt) != (0, 0)]
    barrier = pltpu.get_barrier_semaphore()
    for k, dt in peers:
        pl.semaphore_signal(barrier, inc=1, device_id=at(k, dt), device_id_type=MESH)

    row_i = lax.broadcasted_iota(jnp.int32, (2 * COLS, COLS), 0)
    col_i = lax.broadcasted_iota(jnp.int32, (2 * COLS, COLS), 1)
    for kx in range(3):
        pick[:, kx * COLS : (kx + 1) * COLS] = jnp.where(row_i == 2 * col_i + (kx - 1), 1.0, 0.0).astype(BF16)
    taps[...] = jnp.zeros_like(taps)
    w1f = w1[...].astype(F32)
    for ky in range(3):
        taps[3 * ky : 3 * ky + 3, 0:CH] = w1f[ky]
    w1m[...] = taps[0:COLS, :].T[0:CH, 0:16].astype(BF16)

    def link(section, side):
        place = tile - 1 + side
        inside = jnp.logical_and(place >= 0, place < n_tile - 1)
        place = jnp.clip(place, 0, n_tile - 2)
        section = jnp.clip(section, 0, 2 * n_sec - 1)
        return jnp.where(inside, seam[place, section], 0).astype(F32)

    pl.semaphore_wait(barrier, len(peers))

    def img_copy(k, dt, i):
        dst = own_img if k == 0 else far_img.at[int(k < 0)]
        src, rows = {-1: (img.at[:, 0:16], slice(48, 64)), 0: (img, slice(16, 48)), 1: (img.at[:, 16:32], slice(0, 16))}[dt]
        return pltpu.make_async_remote_copy(
            src_ref=src, dst_ref=dst.at[:, rows], send_sem=img_send.at[i], recv_sem=img_recv.at[i],
            device_id=at(k, dt), device_id_type=MESH,
        )

    img_copies = [img_copy(k, dt, i) for i, (k, dt) in enumerate([p for p in peers if p[0] in (0, -2, 2)])]
    for copy in img_copies:
        copy.start()

    w3m[...] = w3[...]
    for kx in range(3):
        rows = slice(kx * CH, (kx + 1) * CH)
        w2m[rows, :] = jnp.concatenate([w2[ky, kx].astype(F32) for ky in range(3)], axis=1).astype(BF16)
        d2m[rows, :] = jnp.concatenate([d2[ky, kx].astype(F32) for ky in range(3)], axis=1).astype(BF16)
        d1m[rows, :] = jnp.concatenate(
            [d1[ky, kx].astype(F32) for ky in range(3)] + [jnp.zeros((CH, K1 - 3 * DISP), F32)], axis=1
        ).astype(BF16)
    d3m[...] = jnp.zeros_like(d3m)
    for kx in range(3):
        d3m[kx * 8 : kx * 8 + 2, :] = jnp.concatenate([d3[ky, kx].astype(F32) for ky in range(3)], axis=1)
    for n in range(6):
        for y in range(ROWS + 2):
            cost3[n, y * K1 + 240 : y * K1 + K1, :] = jnp.zeros((8, COLS), F32)

    for copy in img_copies[:2]:
        copy.wait_recv()

    base = 2 * sec

    def encode(below, mid, above, lower, upper, rim, write):
        below = dot(below, pick[...]) * lower
        mid = dot(mid, pick[...])
        above = dot(above, pick[...]) * upper
        for kx in range(3):
            cols = slice(kx * COLS, (kx + 1) * COLS)
            taps[pl.ds(kx, 16, stride=3), :] = below[:, cols]
            taps[pl.ds(48 + kx, 32, stride=3), :] = mid[:, cols]
            taps[pl.ds(144 + kx, 16, stride=3), :] = above[:, cols]

        for y in range(-rim - 2, ROWS + rim + 2, 2):
            at_row = 6 * y + 45
            x = jnp.concatenate([taps[at_row : at_row + 16, :], taps[at_row + 6 : at_row + 22, :]], axis=1)
            v = leaky(dot(w1m[...], x.astype(BF16)))
            if y >= ROWS:
                v = v * upper
            v = v.astype(BF16)
            for h in range(2):
                vh = v[:, h * COLS : (h + 1) * COLS]
                for ky in range(3):
                    to = y + h + 2 - 2 * ky
                    if -rim <= to < ROWS + rim:
                        first3[to + RADIUS, ky * CH : (ky + 1) * CH, :] = vh

        for y in range(-rim, ROWS + rim, 2):
            x = jnp.concatenate([first3[y + RADIUS], first3[y + RADIUS + 1]], axis=1)
            o = dot(w2m[...], x)
            z = jnp.concatenate([leaky(fold(o, h, 2, CH)).astype(BF16) for h in range(2)], axis=1)
            d = dot(w3m[...], z).astype(BF16)
            for h in range(2):
                write(y + h, d[:, h * COLS : (h + 1) * COLS])

    def near_copies(s):
        copies = []
        for i, k in enumerate((0, -1, 1)):
            for dt in (-1, 0, 1):
                if (k, dt) == (0, 0):
                    continue
                src, dst = {
                    -1: (slice(RADIUS, 2 * RADIUS), slice(RADIUS + ROWS, EXT)),
                    0: (slice(RADIUS, RADIUS + ROWS), slice(RADIUS, RADIUS + ROWS)),
                    1: (slice(ROWS, RADIUS + ROWS), slice(0, RADIUS)),
                }[dt]
                copies.append(pltpu.make_async_remote_copy(
                    src_ref=held.at[2 + s, src], dst_ref=held.at[2 + s - 2 * k, dst],
                    send_sem=near_send.at[s, 3 * i + dt + 1], recv_sem=near_recv.at[s, 3 * i + dt + 1],
                    device_id=at(k, dt), device_id_type=MESH,
                ))
        return copies

    def encode_own(s, carry):
        def write(y, d):
            held[2 + s, RADIUS + y] = d
            desc_cy[s, pl.ds(y, DESC, stride=ROWS), :] = d.astype(F32)

        encode(own_img[s, 0:16], img[s], own_img[s, 48:64], link(base + s, 0), link(base + s, 1), 0, write)
        for copy in near_copies(s):
            copy.start()
        return carry

    lax.fori_loop(0, 2, encode_own, 0)

    def partner_links(s, j):
        ahead, behind = base + s + OFFSETS[j], base + s - OFFSETS[j]
        flag = partners[s, j] == ahead
        return flag, jnp.where(flag, link(ahead, 0), link(behind, 0)), jnp.where(flag, link(ahead, 1), link(behind, 1))

    for copy in img_copies[2:]:
        copy.wait_recv()

    def encode_far(s, carry):
        flag, lower, upper = partner_links(s, 2)

        def write(y, d):
            d = d.astype(F32)
            if y < 0:
                d = d * lower
            elif y >= ROWS:
                d = d * upper
            far_part[s, pl.ds(y + RADIUS, DESC, stride=EXT), :] = d

        chosen = jnp.where(flag, far_img[1, s].astype(F32), far_img[0, s].astype(F32)).astype(BF16)
        encode(chosen[0:16], chosen[16:48], chosen[48:64], lower, upper, RADIUS, write)
        return carry

    lax.fori_loop(0, 2, encode_far, 0)

    lane = lax.broadcasted_iota(jnp.int32, (COLS, COLS), 1)

    def spread(i, carry):
        s, chunk = i // 4, lax.rem(i, 4)
        rows = pl.ds(pl.multiple_of(chunk * COLS, COLS), COLS)
        own = desc_cy[s, rows, :]
        desc_out[s, pl.ds(chunk * 8, 8)] = own.reshape(8, ROWS, COLS).astype(BF16)
        scaled = own * (1.0 / math.sqrt(DESC))
        for b in range(SPAN):
            d = b - RADIUS
            moved = pltpu.roll(scaled, d % COLS, 1) if d else scaled
            keep = jnp.logical_and(lane - d >= 0, lane - d < COLS)
            own_rot[s, b, rows, :] = jnp.where(keep, moved, 0.0)
        return carry

    lax.fori_loop(0, 8, spread, 0)

    def edge_copy(stage, n, direction):
        if stage == 0:
            src, dst = edge_out.at[n, direction], edge_in.at[n, direction]
        else:
            buf = (hid1, hid2)[stage - 1]
            if direction == 0:
                src, dst = buf.at[n, 1, CH : 2 * CH], buf.at[n, ROWS, 2 * CH : 3 * CH]
            else:
                src, dst = buf.at[n, ROWS, CH : 2 * CH], buf.at[n, 1, 0:CH]
        return pltpu.make_async_remote_copy(
            src_ref=src, dst_ref=dst,
            send_sem=edge_send.at[stage, n, direction], recv_sem=edge_recv.at[stage, n, direction],
            device_id=at(0, 2 * direction - 1), device_id_type=MESH,
        )

    def gather(j, s):
        flag, lower, upper = partner_links(s, j)

        def row(y, carry):
            ahead = held[2 + s + OFFSETS[j], y].astype(F32)
            behind = held[2 + s - OFFSETS[j], y].astype(F32)
            m = jnp.where(y < RADIUS, lower, jnp.where(y >= RADIUS + ROWS, upper, 1.0))
            part[pl.ds(y, DESC, stride=EXT), :] = jnp.where(flag, ahead, behind) * m
            return carry

        lax.fori_loop(0, EXT, row, 0, unroll=4)

    def correlate(j, s, part):
        n = 2 * j + s

        def column(b, carry):
            def channel(c, acc):
                own = own_rot[s, b, pl.ds(pl.multiple_of(c * ROWS, ROWS), ROWS), :]
                start = pl.multiple_of(c * EXT, 8)
                return tuple(acc[a] + own * part[pl.ds(start + a, ROWS), :] for a in range(SPAN))

            acc = lax.fori_loop(
                0, DESC, channel, tuple(jnp.zeros((ROWS, COLS), F32) for _ in range(SPAN)), unroll=4
            )
            shift = lax.rem(COLS + RADIUS - b, COLS)
            for a in range(SPAN):
                moved = pltpu.roll(acc[a], shift, 1)
                d = a * SPAN + b
                for ky in range(3):
                    cost3[n, pl.ds((2 - ky) * K1 + ky * DISP + d, ROWS, stride=K1), :] = moved
            return carry

        lax.fori_loop(0, SPAN, column, 0)
        edge_out[n, 0] = cost3[n, K1 + DISP : K1 + DISP + 88, :]
        edge_out[n, 1] = cost3[n, ROWS * K1 + DISP : ROWS * K1 + DISP + 88, :]
        for direction in (0, 1):
            edge_copy(0, n, direction).start()

    def far_slot(s, carry):
        correlate(2, s, far_part.at[s])
        return carry

    lax.fori_loop(0, 2, far_slot, 0)

    def near_wait(s, carry):
        for copy in near_copies(s):
            copy.wait_recv()
        return carry

    lax.fori_loop(0, 2, near_wait, 0)

    for j in range(2):

        def near_slot(s, carry, j=j):
            gather(j, s)
            correlate(j, s, part)
            return carry

        lax.fori_loop(0, 2, near_slot, 0)

    def hidden_rows(n, q, o, buf):
        for h in range(2):
            v = leaky(fold(o, h, 1, CH)).astype(BF16)
            for ky in range(3):
                buf[n, 2 * q + h + 2 - ky, ky * CH : (ky + 1) * CH, :] = v

    def decode_one(i, carry):
        n = lax.rem(i + 4, 6)
        s = lax.rem(n, 2)
        for direction in (0, 1):
            edge_copy(0, n, direction).wait_recv()
        cost3[n, K1 : K1 + DISP, :] = edge_in[n, 1, 0:DISP, :] * link(base + s, 0)
        cost3[n, ROWS * K1 + 2 * DISP : ROWS * K1 + 3 * DISP, :] = edge_in[n, 0, 0:DISP, :] * link(base + s, 1)

        def rows(q, carry):
            start = pl.multiple_of((2 * q + 1) * K1, 8)
            x = jnp.concatenate([cost3[n, pl.ds(start, K1), :], cost3[n, pl.ds(start + K1, K1), :]], axis=1)
            hidden_rows(n, q, dot(d1m[...], x.astype(BF16)), hid1)
            return carry

        lax.fori_loop(0, ROWS // 2, rows, 0, unroll=8)
        for direction in (0, 1):
            edge_copy(1, n, direction).start()
        return carry

    lax.fori_loop(0, 6, decode_one, 0)

    def rims(stage, n, buf):
        s = lax.rem(n, 2)
        for direction in (0, 1):
            edge_copy(stage, n, direction).wait_recv()
        buf[n, 1, 0:CH, :] = (buf[n, 1, 0:CH, :].astype(F32) * link(base + s, 0)).astype(BF16)
        top = slice(2 * CH, 3 * CH)
        buf[n, ROWS, top, :] = (buf[n, ROWS, top, :].astype(F32) * link(base + s, 1)).astype(BF16)

    def decode_two(i, carry):
        n = lax.rem(i + 4, 6)
        rims(1, n, hid1)

        def rows(q, carry):
            x = jnp.concatenate([hid1[n, 2 * q + 1], hid1[n, 2 * q + 2]], axis=1)
            hidden_rows(n, q, dot(d2m[...], x), hid2)
            return carry

        lax.fori_loop(0, ROWS // 2, rows, 0, unroll=8)
        for direction in (0, 1):
            edge_copy(2, n, direction).start()
        return carry

    lax.fori_loop(0, 6, decode_two, 0)

    def decode_three(i, carry):
        n = lax.rem(i + 4, 6)
        rims(2, n, hid2)
        weights = d3m[...].astype(BF16)

        def rows(q, carry):
            x = jnp.concatenate([hid2[n, 2 * q + 1], hid2[n, 2 * q + 2]], axis=1)
            o = dot(weights, x)
            for h in range(2):
                flow_y[pl.ds(pl.multiple_of((2 * q + h) * 8, 8), 8), :] = fold(o, h, 1, 8)
            return carry

        lax.fori_loop(0, ROWS // 2, rows, 0, unroll=8)
        s, j = lax.rem(n, 2), n // 2
        for o in range(2):
            flow_out[s, j, o] = flow_y[pl.ds(o, ROWS, stride=8), :]
        return carry

    lax.fori_loop(0, 6, decode_three, 0)

    for copy in img_copies:
        copy.wait_send()

    def near_drain(s, carry):
        for copy in near_copies(s):
            copy.wait_send()
        return carry

    lax.fori_loop(0, 2, near_drain, 0)

    def drain(n, carry):
        for stage in range(3):
            for direction in (0, 1):
                edge_copy(stage, n, direction).wait_send()
        return carry

    lax.fori_loop(0, 6, drain, 0)


def solution(mesh):
    n_sec, n_tile = mesh.shape["sec"], mesh.shape["tile"]
    vmem = pl.BlockSpec(memory_space=pltpu.VMEM)
    smem = pl.BlockSpec(memory_space=pltpu.SMEM)
    dma = pltpu.SemaphoreType.DMA

    def shards(images, seam_links, partners, enc_first, enc_second, enc_third, dec_first, dec_second, dec_third):
        taps_first = lambda w: jnp.transpose(w, (2, 3, 0, 1))
        return pl.pallas_call(
            functools.partial(kernel, n_sec, n_tile),
            out_shape=(
                jax.ShapeDtypeStruct((2, DESC, ROWS, COLS), BF16),
                jax.ShapeDtypeStruct((2, 3, 2, ROWS, COLS), F32),
            ),
            in_specs=[smem, smem] + [vmem] * 7,
            out_specs=(vmem, vmem),
            scratch_shapes=[
                pltpu.VMEM((2, 64, 256), BF16),
                pltpu.VMEM((2, 2, 64, 256), BF16),
                pltpu.VMEM((192, COLS), F32),
                pltpu.VMEM((256, 3 * COLS), BF16),
                pltpu.VMEM((CH, 16), BF16),
                pltpu.VMEM((3 * CH, 3 * CH), BF16),
                pltpu.VMEM((DESC, CH), BF16),
                pltpu.VMEM((3 * CH, K1), BF16),
                pltpu.VMEM((3 * CH, 3 * CH), BF16),
                pltpu.VMEM((24, 3 * CH), F32),
                pltpu.VMEM((EXT, 3 * CH, COLS), BF16),
                pltpu.VMEM((2, DESC * ROWS, COLS), F32),
                pltpu.VMEM((2, SPAN, DESC * ROWS, COLS), F32),
                pltpu.VMEM((6, EXT, DESC, COLS), BF16),
                pltpu.VMEM((DESC * EXT, COLS), F32),
                pltpu.VMEM((2, DESC * EXT, COLS), F32),
                pltpu.VMEM((6, (ROWS + 2) * K1, COLS), F32),
                pltpu.VMEM((6, 2, 88, COLS), F32),
                pltpu.VMEM((6, 2, 88, COLS), F32),
                pltpu.VMEM((6, ROWS + 2, 3 * CH, COLS), BF16),
                pltpu.VMEM((6, ROWS + 2, 3 * CH, COLS), BF16),
                pltpu.VMEM((ROWS * 8, COLS), F32),
                dma((8,)), dma((8,)), dma((2, 9)), dma((2, 9)),
                dma((3, 6, 2)), dma((3, 6, 2)),
            ],
            compiler_params=pltpu.CompilerParams(
                collective_id=0, has_side_effects=True, vmem_limit_bytes=56 * 1024 * 1024
            ),
        )(
            jnp.transpose(seam_links), partners, images,
            jnp.transpose(enc_first, (1, 2, 3, 0))[0], taps_first(enc_second), taps_first(enc_third)[0, 0],
            taps_first(dec_first), taps_first(dec_second), taps_first(dec_third),
        )

    return jax.shard_map(
        shards,
        mesh=mesh,
        in_specs=(P("sec", "tile", None), P(), P("sec", None), P(), P(), P(), P(), P(), P()),
        out_specs=(P("sec", None, "tile", None), P("sec", None, None, "tile", None)),
        check_vma=False,
    )
```

```python
import functools
import math

import jax
import jax.numpy as jnp
from jax import lax
from jax.experimental import pallas as pl
from jax.experimental.pallas import tpu as pltpu
from jax.sharding import PartitionSpec as P

MESH = pl.DeviceIdType.MESH
F32, BF16 = jnp.float32, jnp.bfloat16

RADIUS = 4
SPAN = 2 * RADIUS + 1
DISP = SPAN * SPAN
OFFSETS = (1, 2, 4)
ROWS = 16
COLS = 128
CH = 64
DESC = 32
EVEN = DISP - 1
PAD = EVEN + 8
K1 = 3 * EVEN + 8
EXT = ROWS + 2 * RADIUS


def leaky(v):
    return jnp.maximum(v, 0.1 * v)


def dot(a, b):
    return jnp.dot(a, b, preferred_element_type=F32)


def fold(out, half, shift, rows):
    lane = lax.broadcasted_iota(jnp.int32, (rows, COLS), 1)
    cols = slice(half * COLS, (half + 1) * COLS)
    left = pltpu.roll(out[0:rows, cols], shift, 1)
    right = pltpu.roll(out[2 * rows : 3 * rows, cols], COLS - shift, 1)
    return (
        jnp.where(lane >= shift, left, 0.0)
        + out[rows : 2 * rows, cols]
        + jnp.where(lane < COLS - shift, right, 0.0)
    )


def kernel(
    n_sec, n_tile, seam, partners, img, w1, w2, w3, d1, d2, d3, desc_out, flow_out,
    own_img, far_img, taps, pick, w1m, w2m, w3m, d1m, d2m, d3m, first3, second, desc_cy, own_rot, held, part, raw,
    cost, hid1, hid2, flow_y,
    img_send, img_recv, near_send, near_recv, edge_send, edge_recv,
):
    sec, tile = lax.axis_index("sec"), lax.axis_index("tile")

    def at(k, dt):
        return (lax.rem(sec + k + n_sec, n_sec), lax.rem(tile + dt + n_tile, n_tile))

    peers = [(k, dt) for k in (0, -1, 1, -2, 2) for dt in (-1, 0, 1) if (k, dt) != (0, 0)]
    barrier = pltpu.get_barrier_semaphore()
    for k, dt in peers:
        pl.semaphore_signal(barrier, inc=1, device_id=at(k, dt), device_id_type=MESH)

    row_i = lax.broadcasted_iota(jnp.int32, (2 * COLS, COLS), 0)
    col_i = lax.broadcasted_iota(jnp.int32, (2 * COLS, COLS), 1)
    for kx in range(3):
        pick[:, kx * COLS : (kx + 1) * COLS] = jnp.where(row_i == 2 * col_i + (kx - 1), 1.0, 0.0).astype(BF16)
    taps[...] = jnp.zeros_like(taps)
    w1f = w1[...].astype(F32)
    for ky in range(3):
        taps[3 * ky : 3 * ky + 3, 0:CH] = w1f[ky]
    w1m[...] = taps[0:COLS, :].T[0:CH, 0:16].astype(BF16)

    def link(section, side):
        place = tile - 1 + side
        inside = jnp.logical_and(place >= 0, place < n_tile - 1)
        place = jnp.clip(place, 0, n_tile - 2)
        section = jnp.clip(section, 0, 2 * n_sec - 1)
        return jnp.where(inside, seam[place, section], 0).astype(F32)

    pl.semaphore_wait(barrier, len(peers))

    def img_copy(k, dt, i):
        dst = own_img if k == 0 else far_img.at[int(k < 0)]
        src, rows = {-1: (img.at[:, 0:16], slice(48, 64)), 0: (img, slice(16, 48)), 1: (img.at[:, 16:32], slice(0, 16))}[dt]
        return pltpu.make_async_remote_copy(
            src_ref=src, dst_ref=dst.at[:, rows], send_sem=img_send.at[i], recv_sem=img_recv.at[i],
            device_id=at(k, dt), device_id_type=MESH,
        )

    img_copies = [img_copy(k, dt, i) for i, (k, dt) in enumerate([p for p in peers if p[0] in (0, -2, 2)])]
    for copy in img_copies:
        copy.start()

    w3m[...] = w3[...]
    for kx in range(3):
        rows = slice(kx * CH, (kx + 1) * CH)
        w2m[rows, :] = jnp.concatenate([w2[ky, kx].astype(F32) for ky in range(3)], axis=1).astype(BF16)
        d2m[rows, :] = jnp.concatenate([d2[ky, kx].astype(F32) for ky in range(3)], axis=1).astype(BF16)
        d1m[rows, :] = jnp.concatenate(
            [d1[ky, kx].astype(F32)[:, 0:EVEN] for ky in range(3)]
            + [d1[ky, kx].astype(F32)[:, EVEN:DISP] for ky in range(3)]
            + [jnp.zeros((CH, K1 - 3 * DISP), F32)],
            axis=1,
        ).astype(BF16)
    d3m[...] = jnp.zeros_like(d3m)
    for kx in range(3):
        d3m[kx * 8 : kx * 8 + 2, :] = jnp.concatenate([d3[ky, kx].astype(F32) for ky in range(3)], axis=1)
    raw[...] = jnp.zeros_like(raw)
    for n in range(6):
        for y in [*range(1, ROWS + 1), *range(ROWS + 2, ROWS + 7)]:
            cost[n, y * PAD + EVEN : (y + 1) * PAD, :] = jnp.zeros((8, COLS), F32)

    for copy in img_copies[:2]:
        copy.wait_recv()

    base = 2 * sec

    def encode(below, mid, above, lower, upper, rim, write):
        below = dot(below, pick[...]) * lower
        mid = dot(mid, pick[...])
        above = dot(above, pick[...]) * upper
        for kx in range(3):
            cols = slice(kx * COLS, (kx + 1) * COLS)
            taps[pl.ds(kx, 16, stride=3), :] = below[:, cols]
            taps[pl.ds(48 + kx, 32, stride=3), :] = mid[:, cols]
            taps[pl.ds(144 + kx, 16, stride=3), :] = above[:, cols]

        for y in range(-rim - 2, ROWS + rim + 2, 2):
            at_row = 6 * y + 45
            x = jnp.concatenate([taps[at_row : at_row + 16, :], taps[at_row + 6 : at_row + 22, :]], axis=1)
            v = leaky(dot(w1m[...], x.astype(BF16)))
            if y >= ROWS:
                v = v * upper
            v = v.astype(BF16)
            for h in range(2):
                vh = v[:, h * COLS : (h + 1) * COLS]
                for ky in range(3):
                    to = y + h + 2 - 2 * ky
                    if -rim <= to < ROWS + rim:
                        first3[to + RADIUS, ky * CH : (ky + 1) * CH, :] = vh

        for y in range(-rim, ROWS + rim, 2):
            x = jnp.concatenate([first3[y + RADIUS], first3[y + RADIUS + 1]], axis=1)
            o = dot(w2m[...], x)
            for h in range(2):
                second[y + h + RADIUS] = leaky(fold(o, h, 2, CH)).astype(BF16)

        for y in range(-rim, ROWS + rim, 2):
            z = jnp.concatenate([second[y + RADIUS], second[y + RADIUS + 1]], axis=1)
            d = dot(w3m[...], z).astype(BF16)
            for h in range(2):
                write(y + h, d[:, h * COLS : (h + 1) * COLS])

    RIMS = {
        -1: (slice(RADIUS, 2 * RADIUS), slice(RADIUS + ROWS, EXT)),
        0: (slice(RADIUS, RADIUS + ROWS), slice(RADIUS, RADIUS + ROWS)),
        1: (slice(ROWS, RADIUS + ROWS), slice(0, RADIUS)),
    }

    def near_copy(s, k, dt, i):
        src, dst = RIMS[dt]
        return pltpu.make_async_remote_copy(
            src_ref=held.at[2 + s, src], dst_ref=held.at[2 + s - 2 * k, dst],
            send_sem=near_send.at[s, i], recv_sem=near_recv.at[s, i],
            device_id=at(k, dt), device_id_type=MESH,
        )

    def near_copies(s, batch):
        if batch == 0:
            k = 2 * s - 1
            return [near_copy(s, k, dt, dt + 1) for dt in (0, -1, 1)] + [near_copy(s, 0, -1, 3), near_copy(s, 0, 1, 4)]
        return [near_copy(s, 1 - 2 * s, dt, dt + 6) for dt in (0, -1, 1)]

    def encode_own(s, carry):
        def write(y, d):
            held[2 + s, RADIUS + y] = d
            desc_cy[s, pl.ds(y, DESC, stride=ROWS), :] = d.astype(F32)

        encode(own_img[s, 0:16], img[s], own_img[s, 48:64], link(base + s, 0), link(base + s, 1), 0, write)
        for copy in near_copies(s, 0):
            copy.start()
        return carry

    lax.fori_loop(0, 2, encode_own, 0)

    def near_rest(s, carry):
        for copy in near_copies(s, 1):
            copy.start()
        return carry

    lax.fori_loop(0, 2, near_rest, 0)

    def partner_links(s, j):
        ahead, behind = base + s + OFFSETS[j], base + s - OFFSETS[j]
        flag = partners[s, j] == ahead
        return flag, jnp.where(flag, link(ahead, 0), link(behind, 0)), jnp.where(flag, link(ahead, 1), link(behind, 1))

    for copy in img_copies[2:]:
        copy.wait_recv()

    def encode_far(s, carry):
        flag, lower, upper = partner_links(s, 2)

        def write(y, d):
            d = d.astype(F32)
            if y < 0:
                d = d * lower
            elif y >= ROWS:
                d = d * upper
            part[4 + s, pl.ds(y + RADIUS, DESC, stride=EXT), :] = d

        chosen = jnp.where(flag, far_img[1, s].astype(F32), far_img[0, s].astype(F32)).astype(BF16)
        encode(chosen[0:16], chosen[16:48], chosen[48:64], lower, upper, RADIUS, write)
        return carry

    lax.fori_loop(0, 2, encode_far, 0)

    lane = lax.broadcasted_iota(jnp.int32, (COLS, COLS), 1)

    def spread(i, carry):
        s, chunk = i // 4, lax.rem(i, 4)
        rows = pl.ds(pl.multiple_of(chunk * COLS, COLS), COLS)
        own = desc_cy[s, rows, :]
        desc_out[s, pl.ds(chunk * 8, 8)] = own.reshape(8, ROWS, COLS).astype(BF16)
        scaled = own * (1.0 / math.sqrt(DESC))
        for b in range(SPAN):
            d = b - RADIUS
            moved = pltpu.roll(scaled, d % COLS, 1) if d else scaled
            keep = jnp.logical_and(lane - d >= 0, lane - d < COLS)
            own_rot[s, b, rows, :] = jnp.where(keep, moved, 0.0)
        return carry

    lax.fori_loop(0, 8, spread, 0)

    def edge_copy(stage, n, direction):
        if stage == 0:
            at_src, at_dst = ((1, ROWS + 1), (ROWS, 0))[direction]
            src = cost.at[n, at_src * PAD : (at_src + 1) * PAD]
            dst = cost.at[n, at_dst * PAD : (at_dst + 1) * PAD]
        else:
            buf = (hid1, hid2)[stage - 1]
            if direction == 0:
                src, dst = buf.at[n, 1, CH : 2 * CH], buf.at[n, ROWS, 2 * CH : 3 * CH]
            else:
                src, dst = buf.at[n, ROWS, CH : 2 * CH], buf.at[n, 1, 0:CH]
        return pltpu.make_async_remote_copy(
            src_ref=src, dst_ref=dst,
            send_sem=edge_send.at[stage, n, direction], recv_sem=edge_recv.at[stage, n, direction],
            device_id=at(0, 2 * direction - 1), device_id_type=MESH,
        )

    def gather(j, s):
        flag, lower, upper = partner_links(s, j)

        def row(y, carry):
            ahead = held[2 + s + OFFSETS[j], y].astype(F32)
            behind = held[2 + s - OFFSETS[j], y].astype(F32)
            m = jnp.where(y < RADIUS, lower, jnp.where(y >= RADIUS + ROWS, upper, 1.0))
            part[2 * j + s, pl.ds(y, DESC, stride=EXT), :] = jnp.where(flag, ahead, behind) * m
            return carry

        lax.fori_loop(0, EXT, row, 0, unroll=4)

    def near_parts(j):
        for s in range(2):
            for copy in near_copies(s, j):
                copy.wait_recv()
        lax.fori_loop(0, 2, lambda s, carry: (gather(j, s), carry)[1], 0)

    def correlate(i, carry):
        n = lax.rem(i + 4, 6)
        s = lax.rem(n, 2)
        pl.when(i == 2)(lambda: near_parts(0))
        pl.when(i == 4)(lambda: near_parts(1))

        def place(b):
            for a in range(SPAN):
                moved = pltpu.roll(raw[a], lax.rem(COLS + RADIUS - b, COLS), 1)
                cost[n, pl.ds(PAD + a * SPAN + b, ROWS, stride=PAD), :] = moved

        def column(b, carry):
            place(jnp.maximum(b - 1, 0))
            acc = [None] * SPAN
            for c in range(DESC):
                own = own_rot[s, b, c * ROWS : (c + 1) * ROWS, :]
                for a in range(SPAN):
                    term = own * part[n, c * EXT + a : c * EXT + a + ROWS, :]
                    acc[a] = term if c == 0 else acc[a] + term
            for a in range(SPAN):
                raw[a] = acc[a]
            return carry

        lax.fori_loop(0, SPAN, column, 0)
        place(SPAN - 1)
        for direction in (0, 1):
            edge_copy(0, n, direction).start()
        return carry

    def hidden_rows(n, q, o, buf):
        for h in range(2):
            v = leaky(fold(o, h, 1, CH)).astype(BF16)
            for ky in range(3):
                buf[n, 2 * q + h + 2 - ky, ky * CH : (ky + 1) * CH, :] = v

    def decode_one(i, carry):
        n = lax.rem(i + 4, 6)
        s = lax.rem(n, 2)
        for direction in (0, 1):
            edge_copy(0, n, direction).wait_recv()
        cost[n, 0:PAD, :] = cost[n, 0:PAD, :] * link(base + s, 0)
        top = slice((ROWS + 1) * PAD, (ROWS + 2) * PAD)
        cost[n, top, :] = cost[n, top, :] * link(base + s, 1)

        def rows(q, carry):
            taps_of = []
            for h in range(2):
                start = pl.multiple_of((2 * q + h) * PAD, 8)
                taps_of.append(jnp.concatenate(
                    [cost[n, pl.ds(start + ky * PAD, EVEN), :] for ky in range(3)]
                    + [cost[n, pl.ds(start + EVEN, 8, stride=PAD), :]],
                    axis=0,
                ))
            x = jnp.concatenate(taps_of, axis=1)
            hidden_rows(n, q, dot(d1m[...], x.astype(BF16)), hid1)
            return carry

        lax.fori_loop(0, ROWS // 2, rows, 0, unroll=8)
        for direction in (0, 1):
            edge_copy(1, n, direction).start()
        return carry


    def rims(stage, n, buf):
        s = lax.rem(n, 2)
        for direction in (0, 1):
            edge_copy(stage, n, direction).wait_recv()
        buf[n, 1, 0:CH, :] = (buf[n, 1, 0:CH, :].astype(F32) * link(base + s, 0)).astype(BF16)
        top = slice(2 * CH, 3 * CH)
        buf[n, ROWS, top, :] = (buf[n, ROWS, top, :].astype(F32) * link(base + s, 1)).astype(BF16)

    def decode_two(i, carry):
        n = lax.rem(i + 4, 6)
        rims(1, n, hid1)

        def rows(q, carry):
            x = jnp.concatenate([hid1[n, 2 * q + 1], hid1[n, 2 * q + 2]], axis=1)
            hidden_rows(n, q, dot(d2m[...], x), hid2)
            return carry

        lax.fori_loop(0, ROWS // 2, rows, 0, unroll=8)
        for direction in (0, 1):
            edge_copy(2, n, direction).start()
        return carry


    def decode_three(i, carry):
        n = lax.rem(i + 4, 6)
        rims(2, n, hid2)
        weights = d3m[...].astype(BF16)

        def rows(q, carry):
            x = jnp.concatenate([hid2[n, 2 * q + 1], hid2[n, 2 * q + 2]], axis=1)
            o = dot(weights, x)
            for h in range(2):
                flow_y[pl.ds(pl.multiple_of((2 * q + h) * 8, 8), 8), :] = fold(o, h, 1, 8)
            return carry

        lax.fori_loop(0, ROWS // 2, rows, 0, unroll=8)
        s, j = lax.rem(n, 2), n // 2
        for o in range(2):
            flow_out[s, j, o] = flow_y[pl.ds(o, ROWS, stride=8), :]
        return carry


    lax.fori_loop(0, 6, correlate, 0)
    lax.fori_loop(0, 6, decode_one, 0)
    lax.fori_loop(0, 6, decode_two, 0)
    lax.fori_loop(0, 6, decode_three, 0)

    for copy in img_copies:
        copy.wait_send()

    def near_drain(s, carry):
        for copy in near_copies(s, 0) + near_copies(s, 1):
            copy.wait_send()
        return carry

    lax.fori_loop(0, 2, near_drain, 0)

    def drain(n, carry):
        for stage in range(3):
            for direction in (0, 1):
                edge_copy(stage, n, direction).wait_send()
        return carry

    lax.fori_loop(0, 6, drain, 0)


def solution(mesh):
    n_sec, n_tile = mesh.shape["sec"], mesh.shape["tile"]
    vmem = pl.BlockSpec(memory_space=pltpu.VMEM)
    smem = pl.BlockSpec(memory_space=pltpu.SMEM)
    dma = pltpu.SemaphoreType.DMA

    def shards(images, seam_links, partners, enc_first, enc_second, enc_third, dec_first, dec_second, dec_third):
        taps_first = lambda w: jnp.transpose(w, (2, 3, 0, 1))
        return pl.pallas_call(
            functools.partial(kernel, n_sec, n_tile),
            out_shape=(
                jax.ShapeDtypeStruct((2, DESC, ROWS, COLS), BF16),
                jax.ShapeDtypeStruct((2, 3, 2, ROWS, COLS), F32),
            ),
            in_specs=[smem, smem] + [vmem] * 7,
            out_specs=(vmem, vmem),
            scratch_shapes=[
                pltpu.VMEM((2, 64, 256), BF16),
                pltpu.VMEM((2, 2, 64, 256), BF16),
                pltpu.VMEM((192, COLS), F32),
                pltpu.VMEM((256, 3 * COLS), BF16),
                pltpu.VMEM((CH, 16), BF16),
                pltpu.VMEM((3 * CH, 3 * CH), BF16),
                pltpu.VMEM((DESC, CH), BF16),
                pltpu.VMEM((3 * CH, K1), BF16),
                pltpu.VMEM((3 * CH, 3 * CH), BF16),
                pltpu.VMEM((24, 3 * CH), F32),
                pltpu.VMEM((EXT, 3 * CH, COLS), BF16),
                pltpu.VMEM((EXT, CH, COLS), BF16),
                pltpu.VMEM((2, DESC * ROWS, COLS), F32),
                pltpu.VMEM((2, SPAN, DESC * ROWS, COLS), F32),
                pltpu.VMEM((6, EXT, DESC, COLS), BF16),
                pltpu.VMEM((6, DESC * EXT, COLS), F32),
                pltpu.VMEM((SPAN, ROWS, COLS), F32),
                pltpu.VMEM((6, (ROWS + 7) * PAD, COLS), F32),
                pltpu.VMEM((6, ROWS + 2, 3 * CH, COLS), BF16),
                pltpu.VMEM((6, ROWS + 2, 3 * CH, COLS), BF16),
                pltpu.VMEM((ROWS * 8, COLS), F32),
                dma((8,)), dma((8,)), dma((2, 9)), dma((2, 9)),
                dma((3, 6, 2)), dma((3, 6, 2)),
            ],
            compiler_params=pltpu.CompilerParams(
                collective_id=0, has_side_effects=True, vmem_limit_bytes=56 * 1024 * 1024
            ),
        )(
            jnp.transpose(seam_links), partners, images,
            jnp.transpose(enc_first, (1, 2, 3, 0))[0], taps_first(enc_second), taps_first(enc_third)[0, 0],
            taps_first(dec_first), taps_first(dec_second), taps_first(dec_third),
        )

    return jax.shard_map(
        shards,
        mesh=mesh,
        in_specs=(P("sec", "tile", None), P(), P("sec", None), P(), P(), P(), P(), P(), P()),
        out_specs=(P("sec", None, "tile", None), P("sec", None, None, "tile", None)),
        check_vma=False,
    )
```

```python
import functools
import math

import jax
import jax.numpy as jnp
from jax import lax
from jax.experimental import pallas as pl
from jax.experimental.pallas import tpu as pltpu
from jax.sharding import PartitionSpec as P

MESH = pl.DeviceIdType.MESH
F32, BF16 = jnp.float32, jnp.bfloat16

RADIUS = 4
SPAN = 2 * RADIUS + 1
DISP = SPAN * SPAN
OFFSETS = (1, 2, 4)
ROWS = 16
COLS = 128
CH = 64
DESC = 32
EVEN = DISP - 1
PAD = EVEN + 8
K1 = 3 * EVEN + 8
EXT = ROWS + 2 * RADIUS


def leaky(v):
    return jnp.maximum(v, 0.1 * v)


def dot(a, b):
    return jnp.dot(a, b, preferred_element_type=F32)


def fold(out, half, shift, rows):
    lane = lax.broadcasted_iota(jnp.int32, (rows, COLS), 1)
    cols = slice(half * COLS, (half + 1) * COLS)
    left = pltpu.roll(out[0:rows, cols], shift, 1)
    right = pltpu.roll(out[2 * rows : 3 * rows, cols], COLS - shift, 1)
    return (
        jnp.where(lane >= shift, left, 0.0)
        + out[rows : 2 * rows, cols]
        + jnp.where(lane < COLS - shift, right, 0.0)
    )


def kernel(
    n_sec, n_tile, seam, partners, img, w1, w2, w3, d1, d2, d3, desc_out, flow_out,
    own_img, far_img, taps, pick, w1m, w2m, w3m, d1m, d2m, d3m, first3, second, desc_cy, own_rot, held, part, raw,
    cost, hid1, hid2, flow_y,
    img_send, img_recv, near_send, near_recv, edge_send, edge_recv,
):
    sec, tile = lax.axis_index("sec"), lax.axis_index("tile")

    def at(k, dt):
        return (lax.rem(sec + k + n_sec, n_sec), lax.rem(tile + dt + n_tile, n_tile))

    peers = [(k, dt) for k in (0, -1, 1, -2, 2) for dt in (-1, 0, 1) if (k, dt) != (0, 0)]
    barrier = pltpu.get_barrier_semaphore()
    for k, dt in peers:
        pl.semaphore_signal(barrier, inc=1, device_id=at(k, dt), device_id_type=MESH)

    row_i = lax.broadcasted_iota(jnp.int32, (2 * COLS, COLS), 0)
    col_i = lax.broadcasted_iota(jnp.int32, (2 * COLS, COLS), 1)
    for kx in range(3):
        pick[:, kx * COLS : (kx + 1) * COLS] = jnp.where(row_i == 2 * col_i + (kx - 1), 1.0, 0.0).astype(BF16)
    taps[...] = jnp.zeros_like(taps)
    w1f = w1[...].astype(F32)
    for ky in range(3):
        taps[3 * ky : 3 * ky + 3, 0:CH] = w1f[ky]
    w1m[...] = taps[0:COLS, :].T[0:CH, 0:16].astype(BF16)

    def link(section, side):
        place = tile - 1 + side
        inside = jnp.logical_and(place >= 0, place < n_tile - 1)
        place = jnp.clip(place, 0, n_tile - 2)
        section = jnp.clip(section, 0, 2 * n_sec - 1)
        return jnp.where(inside, seam[place, section], 0).astype(F32)

    w3m[...] = w3[...]
    for kx in range(3):
        rows = slice(kx * CH, (kx + 1) * CH)
        w2m[rows, :] = jnp.concatenate([w2[ky, kx].astype(F32) for ky in range(3)], axis=1).astype(BF16)
        d2m[rows, :] = jnp.concatenate([d2[ky, kx].astype(F32) for ky in range(3)], axis=1).astype(BF16)
        d1m[rows, :] = jnp.concatenate(
            [d1[ky, kx].astype(F32)[:, 0:EVEN] for ky in range(3)]
            + [d1[ky, kx].astype(F32)[:, EVEN:DISP] for ky in range(3)]
            + [jnp.zeros((CH, K1 - 3 * DISP), F32)],
            axis=1,
        ).astype(BF16)
    d3m[...] = jnp.zeros_like(d3m)
    for kx in range(3):
        d3m[kx * 8 : kx * 8 + 2, :] = jnp.concatenate([d3[ky, kx].astype(F32) for ky in range(3)], axis=1)
    raw[...] = jnp.zeros_like(raw)
    for n in range(6):
        for y in [*range(1, ROWS + 1), *range(ROWS + 2, ROWS + 7)]:
            cost[n, y * PAD + EVEN : (y + 1) * PAD, :] = jnp.zeros((8, COLS), F32)

    pl.semaphore_wait(barrier, len(peers))

    def img_copy(k, dt, i):
        dst = own_img if k == 0 else far_img.at[int(k < 0)]
        src, rows = {-1: (img.at[:, 0:16], slice(48, 64)), 0: (img, slice(16, 48)), 1: (img.at[:, 16:32], slice(0, 16))}[dt]
        return pltpu.make_async_remote_copy(
            src_ref=src, dst_ref=dst.at[:, rows], send_sem=img_send.at[i], recv_sem=img_recv.at[i],
            device_id=at(k, dt), device_id_type=MESH,
        )

    img_copies = [img_copy(k, dt, i) for i, (k, dt) in enumerate([p for p in peers if p[0] in (0, -2, 2)])]
    for copy in img_copies:
        copy.start()

    for copy in img_copies[:2]:
        copy.wait_recv()

    base = 2 * sec

    def encode(below, mid, above, lower, upper, rim, write):
        below = dot(below, pick[...]) * lower
        mid = dot(mid, pick[...])
        above = dot(above, pick[...]) * upper
        for kx in range(3):
            cols = slice(kx * COLS, (kx + 1) * COLS)
            taps[pl.ds(kx, 16, stride=3), :] = below[:, cols]
            taps[pl.ds(48 + kx, 32, stride=3), :] = mid[:, cols]
            taps[pl.ds(144 + kx, 16, stride=3), :] = above[:, cols]

        for y in range(-rim - 2, ROWS + rim + 2, 2):
            at_row = 6 * y + 45
            x = jnp.concatenate([taps[at_row : at_row + 16, :], taps[at_row + 6 : at_row + 22, :]], axis=1)
            v = leaky(dot(w1m[...], x.astype(BF16)))
            if y >= ROWS:
                v = v * upper
            v = v.astype(BF16)
            for h in range(2):
                vh = v[:, h * COLS : (h + 1) * COLS]
                for ky in range(3):
                    to = y + h + 2 - 2 * ky
                    if -rim <= to < ROWS + rim:
                        first3[to + RADIUS, ky * CH : (ky + 1) * CH, :] = vh

        for y in range(-rim, ROWS + rim, 2):
            x = jnp.concatenate([first3[y + RADIUS], first3[y + RADIUS + 1]], axis=1)
            o = dot(w2m[...], x)
            for h in range(2):
                second[y + h + RADIUS] = leaky(fold(o, h, 2, CH)).astype(BF16)

        for y in range(-rim, ROWS + rim, 2):
            z = jnp.concatenate([second[y + RADIUS], second[y + RADIUS + 1]], axis=1)
            d = dot(w3m[...], z).astype(BF16)
            for h in range(2):
                write(y + h, d[:, h * COLS : (h + 1) * COLS])

    RIMS = {
        -1: (slice(RADIUS, 2 * RADIUS), slice(RADIUS + ROWS, EXT)),
        0: (slice(RADIUS, RADIUS + ROWS), slice(RADIUS, RADIUS + ROWS)),
        1: (slice(ROWS, RADIUS + ROWS), slice(0, RADIUS)),
    }

    def near_copy(s, k, dt, i):
        src, dst = RIMS[dt]
        return pltpu.make_async_remote_copy(
            src_ref=held.at[2 + s, src], dst_ref=held.at[2 + s - 2 * k, dst],
            send_sem=near_send.at[s, i], recv_sem=near_recv.at[s, i],
            device_id=at(k, dt), device_id_type=MESH,
        )

    def near_copies(s, batch):
        if batch == 0:
            k = 2 * s - 1
            return [near_copy(s, k, dt, dt + 1) for dt in (0, -1, 1)] + [near_copy(s, 0, -1, 3), near_copy(s, 0, 1, 4)]
        return [near_copy(s, 1 - 2 * s, dt, dt + 6) for dt in (0, -1, 1)]

    def encode_own(s, carry):
        def write(y, d):
            held[2 + s, RADIUS + y] = d
            desc_cy[s, pl.ds(y, DESC, stride=ROWS), :] = d.astype(F32)

        encode(own_img[s, 0:16], img[s], own_img[s, 48:64], link(base + s, 0), link(base + s, 1), 0, write)
        for copy in near_copies(s, 0):
            copy.start()
        return carry

    lax.fori_loop(0, 2, encode_own, 0)

    def near_rest(s, carry):
        for copy in near_copies(s, 1):
            copy.start()
        return carry

    lax.fori_loop(0, 2, near_rest, 0)

    def partner_links(s, j):
        ahead, behind = base + s + OFFSETS[j], base + s - OFFSETS[j]
        flag = partners[s, j] == ahead
        return flag, jnp.where(flag, link(ahead, 0), link(behind, 0)), jnp.where(flag, link(ahead, 1), link(behind, 1))

    lane = lax.broadcasted_iota(jnp.int32, (COLS, COLS), 1)

    def spread(i, carry):
        s, chunk = i // 4, lax.rem(i, 4)
        rows = pl.ds(pl.multiple_of(chunk * COLS, COLS), COLS)
        own = desc_cy[s, rows, :]
        desc_out[s, pl.ds(chunk * 8, 8)] = own.reshape(8, ROWS, COLS).astype(BF16)
        scaled = own * (1.0 / math.sqrt(DESC))
        for b in range(SPAN):
            d = b - RADIUS
            moved = pltpu.roll(scaled, d % COLS, 1) if d else scaled
            keep = jnp.logical_and(lane - d >= 0, lane - d < COLS)
            own_rot[s, b, rows, :] = jnp.where(keep, moved, 0.0)
        return carry

    lax.fori_loop(0, 8, spread, 0)

    for copy in img_copies[2:]:
        copy.wait_recv()

    def encode_far(s, carry):
        flag, lower, upper = partner_links(s, 2)

        def write(y, d):
            d = d.astype(F32)
            if y < 0:
                d = d * lower
            elif y >= ROWS:
                d = d * upper
            part[4 + s, pl.ds(y + RADIUS, DESC, stride=EXT), :] = d

        chosen = jnp.where(flag, far_img[1, s].astype(F32), far_img[0, s].astype(F32)).astype(BF16)
        encode(chosen[0:16], chosen[16:48], chosen[48:64], lower, upper, RADIUS, write)
        return carry

    lax.fori_loop(0, 2, encode_far, 0)

    def edge_copy(stage, n, direction):
        if stage == 0:
            at_src, at_dst = ((1, ROWS + 1), (ROWS, 0))[direction]
            src = cost.at[n, at_src * PAD : (at_src + 1) * PAD]
            dst = cost.at[n, at_dst * PAD : (at_dst + 1) * PAD]
        else:
            buf = (hid1, hid2)[stage - 1]
            if direction == 0:
                src, dst = buf.at[n, 1, CH : 2 * CH], buf.at[n, ROWS, 2 * CH : 3 * CH]
            else:
                src, dst = buf.at[n, ROWS, CH : 2 * CH], buf.at[n, 1, 0:CH]
        return pltpu.make_async_remote_copy(
            src_ref=src, dst_ref=dst,
            send_sem=edge_send.at[stage, n, direction], recv_sem=edge_recv.at[stage, n, direction],
            device_id=at(0, 2 * direction - 1), device_id_type=MESH,
        )

    def gather(j, s):
        flag, lower, upper = partner_links(s, j)

        def row(y, carry):
            ahead = held[2 + s + OFFSETS[j], y].astype(F32)
            behind = held[2 + s - OFFSETS[j], y].astype(F32)
            m = jnp.where(y < RADIUS, lower, jnp.where(y >= RADIUS + ROWS, upper, 1.0))
            part[2 * j + s, pl.ds(y, DESC, stride=EXT), :] = jnp.where(flag, ahead, behind) * m
            return carry

        lax.fori_loop(0, EXT, row, 0, unroll=4)

    def near_parts(j):
        for s in range(2):
            for copy in near_copies(s, j):
                copy.wait_recv()
        lax.fori_loop(0, 2, lambda s, carry: (gather(j, s), carry)[1], 0)

    def correlate(i, carry):
        n = lax.rem(i + 4, 6)
        s = lax.rem(n, 2)
        pl.when(i == 2)(lambda: near_parts(0))
        pl.when(i == 4)(lambda: near_parts(1))

        def place(b):
            for a in range(SPAN):
                moved = pltpu.roll(raw[a], lax.rem(COLS + RADIUS - b, COLS), 1)
                cost[n, pl.ds(PAD + a * SPAN + b, ROWS, stride=PAD), :] = moved

        def column(b, carry):
            place(jnp.maximum(b - 1, 0))
            acc = [None] * SPAN
            for c in range(DESC):
                own = own_rot[s, b, c * ROWS : (c + 1) * ROWS, :]
                for a in range(SPAN):
                    term = own * part[n, c * EXT + a : c * EXT + a + ROWS, :]
                    acc[a] = term if c == 0 else acc[a] + term
            for a in range(SPAN):
                raw[a] = acc[a]
            return carry

        lax.fori_loop(0, SPAN, column, 0)
        place(SPAN - 1)
        for direction in (0, 1):
            edge_copy(0, n, direction).start()
        return carry

    def hidden_rows(n, q, o, buf):
        for h in range(2):
            v = leaky(fold(o, h, 1, CH)).astype(BF16)
            for ky in range(3):
                buf[n, 2 * q + h + 2 - ky, ky * CH : (ky + 1) * CH, :] = v

    def decode_one(i, carry):
        n = lax.rem(i + 4, 6)
        s = lax.rem(n, 2)
        for direction in (0, 1):
            edge_copy(0, n, direction).wait_recv()
        cost[n, 0:PAD, :] = cost[n, 0:PAD, :] * link(base + s, 0)
        top = slice((ROWS + 1) * PAD, (ROWS + 2) * PAD)
        cost[n, top, :] = cost[n, top, :] * link(base + s, 1)

        def rows(q, carry):
            taps_of = []
            for h in range(2):
                start = pl.multiple_of((2 * q + h) * PAD, 8)
                taps_of.append(jnp.concatenate(
                    [cost[n, pl.ds(start + ky * PAD, EVEN), :] for ky in range(3)]
                    + [cost[n, pl.ds(start + EVEN, 8, stride=PAD), :]],
                    axis=0,
                ))
            x = jnp.concatenate(taps_of, axis=1)
            hidden_rows(n, q, dot(d1m[...], x.astype(BF16)), hid1)
            return carry

        lax.fori_loop(0, ROWS // 2, rows, 0, unroll=8)
        for direction in (0, 1):
            edge_copy(1, n, direction).start()
        return carry


    def rims(stage, n, buf):
        s = lax.rem(n, 2)
        for direction in (0, 1):
            edge_copy(stage, n, direction).wait_recv()
        buf[n, 1, 0:CH, :] = (buf[n, 1, 0:CH, :].astype(F32) * link(base + s, 0)).astype(BF16)
        top = slice(2 * CH, 3 * CH)
        buf[n, ROWS, top, :] = (buf[n, ROWS, top, :].astype(F32) * link(base + s, 1)).astype(BF16)

    def decode_two(i, carry):
        n = lax.rem(i + 4, 6)
        rims(1, n, hid1)

        def rows(q, carry):
            x = jnp.concatenate([hid1[n, 2 * q + 1], hid1[n, 2 * q + 2]], axis=1)
            hidden_rows(n, q, dot(d2m[...], x), hid2)
            return carry

        lax.fori_loop(0, ROWS // 2, rows, 0, unroll=8)
        for direction in (0, 1):
            edge_copy(2, n, direction).start()
        return carry


    def decode_three(i, carry):
        n = lax.rem(i + 4, 6)
        rims(2, n, hid2)
        weights = d3m[...].astype(BF16)

        def rows(q, carry):
            x = jnp.concatenate([hid2[n, 2 * q + 1], hid2[n, 2 * q + 2]], axis=1)
            o = dot(weights, x)
            for h in range(2):
                flow_y[pl.ds(pl.multiple_of((2 * q + h) * 8, 8), 8), :] = fold(o, h, 1, 8)
            return carry

        lax.fori_loop(0, ROWS // 2, rows, 0, unroll=8)
        s, j = lax.rem(n, 2), n // 2
        for o in range(2):
            flow_out[s, j, o] = flow_y[pl.ds(o, ROWS, stride=8), :]
        return carry


    lax.fori_loop(0, 6, correlate, 0)
    lax.fori_loop(0, 6, decode_one, 0)
    lax.fori_loop(0, 6, decode_two, 0)
    lax.fori_loop(0, 6, decode_three, 0)

    for copy in img_copies:
        copy.wait_send()

    def near_drain(s, carry):
        for copy in near_copies(s, 0) + near_copies(s, 1):
            copy.wait_send()
        return carry

    lax.fori_loop(0, 2, near_drain, 0)

    def drain(n, carry):
        for stage in range(3):
            for direction in (0, 1):
                edge_copy(stage, n, direction).wait_send()
        return carry

    lax.fori_loop(0, 6, drain, 0)


def solution(mesh):
    n_sec, n_tile = mesh.shape["sec"], mesh.shape["tile"]
    vmem = pl.BlockSpec(memory_space=pltpu.VMEM)
    smem = pl.BlockSpec(memory_space=pltpu.SMEM)
    dma = pltpu.SemaphoreType.DMA

    def shards(images, seam_links, partners, enc_first, enc_second, enc_third, dec_first, dec_second, dec_third):
        taps_first = lambda w: jnp.transpose(w, (2, 3, 0, 1))
        return pl.pallas_call(
            functools.partial(kernel, n_sec, n_tile),
            out_shape=(
                jax.ShapeDtypeStruct((2, DESC, ROWS, COLS), BF16),
                jax.ShapeDtypeStruct((2, 3, 2, ROWS, COLS), F32),
            ),
            in_specs=[smem, smem] + [vmem] * 7,
            out_specs=(vmem, vmem),
            scratch_shapes=[
                pltpu.VMEM((2, 64, 256), BF16),
                pltpu.VMEM((2, 2, 64, 256), BF16),
                pltpu.VMEM((192, COLS), F32),
                pltpu.VMEM((256, 3 * COLS), BF16),
                pltpu.VMEM((CH, 16), BF16),
                pltpu.VMEM((3 * CH, 3 * CH), BF16),
                pltpu.VMEM((DESC, CH), BF16),
                pltpu.VMEM((3 * CH, K1), BF16),
                pltpu.VMEM((3 * CH, 3 * CH), BF16),
                pltpu.VMEM((24, 3 * CH), F32),
                pltpu.VMEM((EXT, 3 * CH, COLS), BF16),
                pltpu.VMEM((EXT, CH, COLS), BF16),
                pltpu.VMEM((2, DESC * ROWS, COLS), F32),
                pltpu.VMEM((2, SPAN, DESC * ROWS, COLS), F32),
                pltpu.VMEM((6, EXT, DESC, COLS), BF16),
                pltpu.VMEM((6, DESC * EXT, COLS), F32),
                pltpu.VMEM((SPAN, ROWS, COLS), F32),
                pltpu.VMEM((6, (ROWS + 7) * PAD, COLS), F32),
                pltpu.VMEM((6, ROWS + 2, 3 * CH, COLS), BF16),
                pltpu.VMEM((6, ROWS + 2, 3 * CH, COLS), BF16),
                pltpu.VMEM((ROWS * 8, COLS), F32),
                dma((8,)), dma((8,)), dma((2, 9)), dma((2, 9)),
                dma((3, 6, 2)), dma((3, 6, 2)),
            ],
            compiler_params=pltpu.CompilerParams(
                collective_id=0, has_side_effects=True, vmem_limit_bytes=56 * 1024 * 1024
            ),
        )(
            jnp.transpose(seam_links), partners, images,
            jnp.transpose(enc_first, (1, 2, 3, 0))[0], taps_first(enc_second), taps_first(enc_third)[0, 0],
            taps_first(dec_first), taps_first(dec_second), taps_first(dec_third),
        )

    return jax.shard_map(
        shards,
        mesh=mesh,
        in_specs=(P("sec", "tile", None), P(), P("sec", None), P(), P(), P(), P(), P(), P()),
        out_specs=(P("sec", None, "tile", None), P("sec", None, None, "tile", None)),
        check_vma=False,
    )
```

```python
import functools
import math

import jax
import jax.numpy as jnp
from jax import lax
from jax.experimental import pallas as pl
from jax.experimental.pallas import tpu as pltpu
from jax.sharding import PartitionSpec as P

MESH = pl.DeviceIdType.MESH
F32, BF16 = jnp.float32, jnp.bfloat16

RADIUS = 4
SPAN = 2 * RADIUS + 1
DISP = SPAN * SPAN
OFFSETS = (1, 2, 4)
ROWS = 16
COLS = 128
CH = 64
DESC = 32
EVEN = DISP - 1
PAD = EVEN + 8
K1 = 3 * EVEN + 8
EXT = ROWS + 2 * RADIUS


def leaky(v):
    return jnp.maximum(v, 0.1 * v)


def dot(a, b):
    return jnp.dot(a, b, preferred_element_type=F32)


def fold(out, half, shift, rows):
    lane = lax.broadcasted_iota(jnp.int32, (rows, COLS), 1)
    cols = slice(half * COLS, (half + 1) * COLS)
    left = pltpu.roll(out[0:rows, cols], shift, 1)
    right = pltpu.roll(out[2 * rows : 3 * rows, cols], COLS - shift, 1)
    return (
        jnp.where(lane >= shift, left, 0.0)
        + out[rows : 2 * rows, cols]
        + jnp.where(lane < COLS - shift, right, 0.0)
    )


def kernel(
    n_sec, n_tile, seam, partners, img, w1, w2, w3, d1, d2, d3, desc_out, flow_out,
    own_img, far_img, taps, pick, w1m, w2m, w3m, d1m, d2m, d3m, first3, second, desc_cy, own_rot, held, part, raw,
    cost, hid1, hid2, flow_y,
    img_send, img_recv, near_send, near_recv, edge_send, edge_recv,
):
    sec, tile = lax.axis_index("sec"), lax.axis_index("tile")

    def at(k, dt):
        return (lax.rem(sec + k + n_sec, n_sec), lax.rem(tile + dt + n_tile, n_tile))

    peers = [(k, dt) for k in (0, -1, 1, -2, 2) for dt in (-1, 0, 1) if (k, dt) != (0, 0)]
    barrier = pltpu.get_barrier_semaphore()
    for k, dt in peers:
        pl.semaphore_signal(barrier, inc=1, device_id=at(k, dt), device_id_type=MESH)

    row_i = lax.broadcasted_iota(jnp.int32, (2 * COLS, COLS), 0)
    col_i = lax.broadcasted_iota(jnp.int32, (2 * COLS, COLS), 1)
    for kx in range(3):
        pick[:, kx * COLS : (kx + 1) * COLS] = jnp.where(row_i == 2 * col_i + (kx - 1), 1.0, 0.0).astype(BF16)
    taps[...] = jnp.zeros_like(taps)
    w1f = w1[...].astype(F32)
    for ky in range(3):
        taps[3 * ky : 3 * ky + 3, 0:CH] = w1f[ky]
    w1m[...] = taps[0:COLS, :].T[0:CH, 0:16].astype(BF16)

    def link(section, side):
        place = tile - 1 + side
        inside = jnp.logical_and(place >= 0, place < n_tile - 1)
        place = jnp.clip(place, 0, n_tile - 2)
        section = jnp.clip(section, 0, 2 * n_sec - 1)
        return jnp.where(inside, seam[place, section], 0).astype(F32)

    w3m[...] = w3[...]
    for kx in range(3):
        rows = slice(kx * CH, (kx + 1) * CH)
        w2m[rows, :] = jnp.concatenate([w2[ky, kx].astype(F32) for ky in range(3)], axis=1).astype(BF16)
        d2m[rows, :] = jnp.concatenate([d2[ky, kx].astype(F32) for ky in range(3)], axis=1).astype(BF16)
        d1m[rows, :] = jnp.concatenate(
            [d1[ky, kx].astype(F32)[:, 0:EVEN] for ky in range(3)]
            + [d1[ky, kx].astype(F32)[:, EVEN:DISP] for ky in range(3)]
            + [jnp.zeros((CH, K1 - 3 * DISP), F32)],
            axis=1,
        ).astype(BF16)
    d3m[...] = jnp.zeros_like(d3m)
    for kx in range(3):
        d3m[kx * 8 : kx * 8 + 2, :] = jnp.concatenate([d3[ky, kx].astype(F32) for ky in range(3)], axis=1)
    raw[...] = jnp.zeros_like(raw)
    for n in range(6):
        for y in [*range(1, ROWS + 1), *range(ROWS + 2, ROWS + 7)]:
            cost[n, y * PAD + EVEN : (y + 1) * PAD, :] = jnp.zeros((8, COLS), F32)

    pl.semaphore_wait(barrier, len(peers))

    def img_copy(k, dt, i):
        dst = own_img if k == 0 else far_img.at[int(k < 0)]
        src, rows = {-1: (img.at[:, 0:16], slice(48, 64)), 0: (img, slice(16, 48)), 1: (img.at[:, 16:32], slice(0, 16))}[dt]
        return pltpu.make_async_remote_copy(
            src_ref=src, dst_ref=dst.at[:, rows], send_sem=img_send.at[i], recv_sem=img_recv.at[i],
            device_id=at(k, dt), device_id_type=MESH,
        )

    img_copies = [img_copy(k, dt, i) for i, (k, dt) in enumerate([p for p in peers if p[0] in (0, -2, 2)])]
    for copy in img_copies:
        copy.start()

    for copy in img_copies[:2]:
        copy.wait_recv()

    base = 2 * sec

    def encode(below, mid, above, lower, upper, rim, write):
        below = dot(below, pick[...]) * lower
        mid = dot(mid, pick[...])
        above = dot(above, pick[...]) * upper
        for kx in range(3):
            cols = slice(kx * COLS, (kx + 1) * COLS)
            taps[pl.ds(kx, 16, stride=3), :] = below[:, cols]
            taps[pl.ds(48 + kx, 32, stride=3), :] = mid[:, cols]
            taps[pl.ds(144 + kx, 16, stride=3), :] = above[:, cols]

        for y in range(-rim - 2, ROWS + rim + 2, 2):
            at_row = 6 * y + 45
            x = jnp.concatenate([taps[at_row : at_row + 16, :], taps[at_row + 6 : at_row + 22, :]], axis=1)
            v = leaky(dot(w1m[...], x.astype(BF16)))
            if y >= ROWS:
                v = v * upper
            v = v.astype(BF16)
            for h in range(2):
                vh = v[:, h * COLS : (h + 1) * COLS]
                for ky in range(3):
                    to = y + h + 2 - 2 * ky
                    if -rim <= to < ROWS + rim:
                        first3[to + RADIUS, ky * CH : (ky + 1) * CH, :] = vh

        for y in range(-rim, ROWS + rim, 2):
            x = jnp.concatenate([first3[y + RADIUS], first3[y + RADIUS + 1]], axis=1)
            o = dot(w2m[...], x)
            for h in range(2):
                second[y + h + RADIUS] = leaky(fold(o, h, 2, CH)).astype(BF16)

        for y in range(-rim, ROWS + rim, 2):
            z = jnp.concatenate([second[y + RADIUS], second[y + RADIUS + 1]], axis=1)
            d = dot(w3m[...], z).astype(BF16)
            for h in range(2):
                write(y + h, d[:, h * COLS : (h + 1) * COLS])

    RIMS = {
        -1: (slice(RADIUS, 2 * RADIUS), slice(RADIUS + ROWS, EXT)),
        0: (slice(RADIUS, RADIUS + ROWS), slice(RADIUS, RADIUS + ROWS)),
        1: (slice(ROWS, RADIUS + ROWS), slice(0, RADIUS)),
    }

    def near_copy(s, k, dt, i):
        src, dst = RIMS[dt]
        return pltpu.make_async_remote_copy(
            src_ref=held.at[2 + s, src], dst_ref=held.at[2 + s - 2 * k, dst],
            send_sem=near_send.at[s, i], recv_sem=near_recv.at[s, i],
            device_id=at(k, dt), device_id_type=MESH,
        )

    def near_copies(s, batch):
        if batch == 0:
            k = 2 * s - 1
            return [near_copy(s, k, dt, dt + 1) for dt in (0, -1, 1)] + [near_copy(s, 0, -1, 3), near_copy(s, 0, 1, 4)]
        return [near_copy(s, 1 - 2 * s, dt, dt + 6) for dt in (0, -1, 1)]

    def encode_own(s, carry):
        def write(y, d):
            held[2 + s, RADIUS + y] = d
            desc_cy[s, pl.ds(y, DESC, stride=ROWS), :] = d.astype(F32)

        encode(own_img[s, 0:16], img[s], own_img[s, 48:64], link(base + s, 0), link(base + s, 1), 0, write)
        for copy in near_copies(s, 0):
            copy.start()
        return carry

    lax.fori_loop(0, 2, encode_own, 0)

    def near_rest(s, carry):
        for copy in near_copies(s, 1):
            copy.start()
        return carry

    lax.fori_loop(0, 2, near_rest, 0)

    def partner_links(s, j):
        ahead, behind = base + s + OFFSETS[j], base + s - OFFSETS[j]
        flag = partners[s, j] == ahead
        return flag, jnp.where(flag, link(ahead, 0), link(behind, 0)), jnp.where(flag, link(ahead, 1), link(behind, 1))

    lane = lax.broadcasted_iota(jnp.int32, (COLS, COLS), 1)

    def spread(i, carry):
        s, chunk = i // 4, lax.rem(i, 4)
        rows = pl.ds(pl.multiple_of(chunk * COLS, COLS), COLS)
        own = desc_cy[s, rows, :]
        desc_out[s, pl.ds(chunk * 8, 8)] = own.reshape(8, ROWS, COLS).astype(BF16)
        scaled = own * (1.0 / math.sqrt(DESC))
        for b in range(SPAN):
            d = b - RADIUS
            moved = pltpu.roll(scaled, d % COLS, 1) if d else scaled
            keep = jnp.logical_and(lane - d >= 0, lane - d < COLS)
            own_rot[s, b, rows, :] = jnp.where(keep, moved, 0.0)
        return carry

    lax.fori_loop(0, 8, spread, 0)

    for copy in img_copies[2:]:
        copy.wait_recv()

    def encode_far(s, carry):
        flag, lower, upper = partner_links(s, 2)

        def write(y, d):
            d = d.astype(F32)
            if y < 0:
                d = d * lower
            elif y >= ROWS:
                d = d * upper
            part[4 + s, pl.ds(y + RADIUS, DESC, stride=EXT), :] = d

        chosen = jnp.where(flag, far_img[1, s].astype(F32), far_img[0, s].astype(F32)).astype(BF16)
        encode(chosen[0:16], chosen[16:48], chosen[48:64], lower, upper, RADIUS, write)
        return carry

    lax.fori_loop(0, 2, encode_far, 0)

    def edge_copy(stage, n, direction):
        if stage == 0:
            at_src, at_dst = ((1, ROWS + 1), (ROWS, 0))[direction]
            src = cost.at[n, at_src * PAD : (at_src + 1) * PAD]
            dst = cost.at[n, at_dst * PAD : (at_dst + 1) * PAD]
        else:
            buf = (hid1, hid2)[stage - 1]
            if direction == 0:
                src, dst = buf.at[n, 1, CH : 2 * CH], buf.at[n, ROWS, 2 * CH : 3 * CH]
            else:
                src, dst = buf.at[n, ROWS, CH : 2 * CH], buf.at[n, 1, 0:CH]
        return pltpu.make_async_remote_copy(
            src_ref=src, dst_ref=dst,
            send_sem=edge_send.at[stage, n, direction], recv_sem=edge_recv.at[stage, n, direction],
            device_id=at(0, 2 * direction - 1), device_id_type=MESH,
        )

    def gather(j, s):
        flag, lower, upper = partner_links(s, j)

        def row(y, carry):
            ahead = held[2 + s + OFFSETS[j], y].astype(F32)
            behind = held[2 + s - OFFSETS[j], y].astype(F32)
            m = jnp.where(y < RADIUS, lower, jnp.where(y >= RADIUS + ROWS, upper, 1.0))
            part[2 * j + s, pl.ds(y, DESC, stride=EXT), :] = jnp.where(flag, ahead, behind) * m
            return carry

        lax.fori_loop(0, EXT, row, 0, unroll=4)

    def near_parts(j):
        for s in range(2):
            for copy in near_copies(s, j):
                copy.wait_recv()
        lax.fori_loop(0, 2, lambda s, carry: (gather(j, s), carry)[1], 0)

    def correlate(i, carry):
        n = lax.rem(i + 4, 6)
        s = lax.rem(n, 2)
        pl.when(i == 2)(lambda: near_parts(0))
        pl.when(i == 4)(lambda: near_parts(1))

        def place(b):
            for a in range(SPAN):
                moved = pltpu.roll(raw[a], lax.rem(COLS + RADIUS - b, COLS), 1)
                cost[n, pl.ds(PAD + a * SPAN + b, ROWS, stride=PAD), :] = moved

        def column(b, carry):
            place(jnp.maximum(b - 1, 0))
            acc = [None] * SPAN
            for c in range(DESC):
                own = own_rot[s, b, c * ROWS : (c + 1) * ROWS, :]
                for a in range(SPAN):
                    term = own * part[n, c * EXT + a : c * EXT + a + ROWS, :]
                    acc[a] = term if c == 0 else acc[a] + term
            for a in range(SPAN):
                raw[a] = acc[a]
            return carry

        lax.fori_loop(0, SPAN, column, 0, unroll=3)
        place(SPAN - 1)
        for direction in (0, 1):
            edge_copy(0, n, direction).start()
        return carry

    def hidden_rows(n, q, o, buf):
        for h in range(2):
            v = leaky(fold(o, h, 1, CH)).astype(BF16)
            for ky in range(3):
                buf[n, 2 * q + h + 2 - ky, ky * CH : (ky + 1) * CH, :] = v

    def decode_one(i, carry):
        n = lax.rem(i + 4, 6)
        s = lax.rem(n, 2)
        for direction in (0, 1):
            edge_copy(0, n, direction).wait_recv()
        cost[n, 0:PAD, :] = cost[n, 0:PAD, :] * link(base + s, 0)
        top = slice((ROWS + 1) * PAD, (ROWS + 2) * PAD)
        cost[n, top, :] = cost[n, top, :] * link(base + s, 1)

        def rows(q, carry):
            taps_of = []
            for h in range(2):
                start = pl.multiple_of((2 * q + h) * PAD, 8)
                taps_of.append(jnp.concatenate(
                    [cost[n, pl.ds(start + ky * PAD, EVEN), :] for ky in range(3)]
                    + [cost[n, pl.ds(start + EVEN, 8, stride=PAD), :]],
                    axis=0,
                ))
            x = jnp.concatenate(taps_of, axis=1)
            hidden_rows(n, q, dot(d1m[...], x.astype(BF16)), hid1)
            return carry

        lax.fori_loop(0, ROWS // 2, rows, 0, unroll=8)
        for direction in (0, 1):
            edge_copy(1, n, direction).start()
        return carry


    def rims(stage, n, buf):
        s = lax.rem(n, 2)
        for direction in (0, 1):
            edge_copy(stage, n, direction).wait_recv()
        buf[n, 1, 0:CH, :] = (buf[n, 1, 0:CH, :].astype(F32) * link(base + s, 0)).astype(BF16)
        top = slice(2 * CH, 3 * CH)
        buf[n, ROWS, top, :] = (buf[n, ROWS, top, :].astype(F32) * link(base + s, 1)).astype(BF16)

    def decode_two(i, carry):
        n = lax.rem(i + 4, 6)
        rims(1, n, hid1)

        def rows(q, carry):
            x = jnp.concatenate([hid1[n, 2 * q + 1], hid1[n, 2 * q + 2]], axis=1)
            hidden_rows(n, q, dot(d2m[...], x), hid2)
            return carry

        lax.fori_loop(0, ROWS // 2, rows, 0, unroll=8)
        for direction in (0, 1):
            edge_copy(2, n, direction).start()
        return carry


    def decode_three(i, carry):
        n = lax.rem(i + 4, 6)
        rims(2, n, hid2)
        weights = d3m[...].astype(BF16)

        def rows(q, carry):
            x = jnp.concatenate([hid2[n, 2 * q + 1], hid2[n, 2 * q + 2]], axis=1)
            o = dot(weights, x)
            for h in range(2):
                flow_y[pl.ds(pl.multiple_of((2 * q + h) * 8, 8), 8), :] = fold(o, h, 1, 8)
            return carry

        lax.fori_loop(0, ROWS // 2, rows, 0, unroll=8)
        s, j = lax.rem(n, 2), n // 2
        for o in range(2):
            flow_out[s, j, o] = flow_y[pl.ds(o, ROWS, stride=8), :]
        return carry


    lax.fori_loop(0, 6, correlate, 0)
    lax.fori_loop(0, 6, decode_one, 0)
    lax.fori_loop(0, 6, decode_two, 0)
    lax.fori_loop(0, 6, decode_three, 0)

    for copy in img_copies:
        copy.wait_send()

    def near_drain(s, carry):
        for copy in near_copies(s, 0) + near_copies(s, 1):
            copy.wait_send()
        return carry

    lax.fori_loop(0, 2, near_drain, 0)

    def drain(n, carry):
        for stage in range(3):
            for direction in (0, 1):
                edge_copy(stage, n, direction).wait_send()
        return carry

    lax.fori_loop(0, 6, drain, 0)


def solution(mesh):
    n_sec, n_tile = mesh.shape["sec"], mesh.shape["tile"]
    vmem = pl.BlockSpec(memory_space=pltpu.VMEM)
    smem = pl.BlockSpec(memory_space=pltpu.SMEM)
    dma = pltpu.SemaphoreType.DMA

    def shards(images, seam_links, partners, enc_first, enc_second, enc_third, dec_first, dec_second, dec_third):
        taps_first = lambda w: jnp.transpose(w, (2, 3, 0, 1))
        return pl.pallas_call(
            functools.partial(kernel, n_sec, n_tile),
            out_shape=(
                jax.ShapeDtypeStruct((2, DESC, ROWS, COLS), BF16),
                jax.ShapeDtypeStruct((2, 3, 2, ROWS, COLS), F32),
            ),
            in_specs=[smem, smem] + [vmem] * 7,
            out_specs=(vmem, vmem),
            scratch_shapes=[
                pltpu.VMEM((2, 64, 256), BF16),
                pltpu.VMEM((2, 2, 64, 256), BF16),
                pltpu.VMEM((192, COLS), F32),
                pltpu.VMEM((256, 3 * COLS), BF16),
                pltpu.VMEM((CH, 16), BF16),
                pltpu.VMEM((3 * CH, 3 * CH), BF16),
                pltpu.VMEM((DESC, CH), BF16),
                pltpu.VMEM((3 * CH, K1), BF16),
                pltpu.VMEM((3 * CH, 3 * CH), BF16),
                pltpu.VMEM((24, 3 * CH), F32),
                pltpu.VMEM((EXT, 3 * CH, COLS), BF16),
                pltpu.VMEM((EXT, CH, COLS), BF16),
                pltpu.VMEM((2, DESC * ROWS, COLS), F32),
                pltpu.VMEM((2, SPAN, DESC * ROWS, COLS), F32),
                pltpu.VMEM((6, EXT, DESC, COLS), BF16),
                pltpu.VMEM((6, DESC * EXT, COLS), F32),
                pltpu.VMEM((SPAN, ROWS, COLS), F32),
                pltpu.VMEM((6, (ROWS + 7) * PAD, COLS), F32),
                pltpu.VMEM((6, ROWS + 2, 3 * CH, COLS), BF16),
                pltpu.VMEM((6, ROWS + 2, 3 * CH, COLS), BF16),
                pltpu.VMEM((ROWS * 8, COLS), F32),
                dma((8,)), dma((8,)), dma((2, 9)), dma((2, 9)),
                dma((3, 6, 2)), dma((3, 6, 2)),
            ],
            compiler_params=pltpu.CompilerParams(
                collective_id=0, has_side_effects=True, vmem_limit_bytes=56 * 1024 * 1024
            ),
        )(
            jnp.transpose(seam_links), partners, images,
            jnp.transpose(enc_first, (1, 2, 3, 0))[0], taps_first(enc_second), taps_first(enc_third)[0, 0],
            taps_first(dec_first), taps_first(dec_second), taps_first(dec_third),
        )

    return jax.shard_map(
        shards,
        mesh=mesh,
        in_specs=(P("sec", "tile", None), P(), P("sec", None), P(), P(), P(), P(), P(), P()),
        out_specs=(P("sec", None, "tile", None), P("sec", None, None, "tile", None)),
        check_vma=False,
    )
```

```python
import functools
import math

import jax
import jax.numpy as jnp
from jax import lax
from jax.experimental import pallas as pl
from jax.experimental.pallas import tpu as pltpu
from jax.sharding import PartitionSpec as P

MESH = pl.DeviceIdType.MESH
F32, BF16 = jnp.float32, jnp.bfloat16

RADIUS = 4
SPAN = 2 * RADIUS + 1
DISP = SPAN * SPAN
OFFSETS = (1, 2, 4)
ROWS = 16
COLS = 128
CH = 64
DESC = 32
EVEN = DISP - 1
PAD = EVEN + 8
K1 = 3 * EVEN + 8
EXT = ROWS + 2 * RADIUS


def leaky(v):
    return jnp.maximum(v, 0.1 * v)


def dot(a, b):
    return jnp.dot(a, b, preferred_element_type=F32)


def fold(out, half, shift, rows):
    lane = lax.broadcasted_iota(jnp.int32, (rows, COLS), 1)
    cols = slice(half * COLS, (half + 1) * COLS)
    left = pltpu.roll(out[0:rows, cols], shift, 1)
    right = pltpu.roll(out[2 * rows : 3 * rows, cols], COLS - shift, 1)
    return (
        jnp.where(lane >= shift, left, 0.0)
        + out[rows : 2 * rows, cols]
        + jnp.where(lane < COLS - shift, right, 0.0)
    )


def kernel(
    n_sec, n_tile, seam, partners, img, w1, w2, w3, d1, d2, d3, desc_out, flow_out,
    own_img, far_img, taps, pick, w1m, w2m, w3m, d1m, d2m, d3m, first3, second, desc_cy, own_rot, held, part, raw,
    cost, hid1, hid2, flow_y,
    img_send, img_recv, near_send, near_recv, edge_send, edge_recv,
):
    sec, tile = lax.axis_index("sec"), lax.axis_index("tile")

    def at(k, dt):
        return (lax.rem(sec + k + n_sec, n_sec), lax.rem(tile + dt + n_tile, n_tile))

    peers = [(k, dt) for k in (0, -1, 1, -2, 2) for dt in (-1, 0, 1) if (k, dt) != (0, 0)]
    barrier = pltpu.get_barrier_semaphore()
    for k, dt in peers:
        pl.semaphore_signal(barrier, inc=1, device_id=at(k, dt), device_id_type=MESH)

    row_i = lax.broadcasted_iota(jnp.int32, (2 * COLS, COLS), 0)
    col_i = lax.broadcasted_iota(jnp.int32, (2 * COLS, COLS), 1)
    for kx in range(3):
        pick[:, kx * COLS : (kx + 1) * COLS] = jnp.where(row_i == 2 * col_i + (kx - 1), 1.0, 0.0).astype(BF16)
    taps[...] = jnp.zeros_like(taps)
    w1f = w1[...].astype(F32)
    for ky in range(3):
        taps[3 * ky : 3 * ky + 3, 0:CH] = w1f[ky]
    w1m[...] = taps[0:COLS, :].T[0:CH, 0:16].astype(BF16)

    def link(section, side):
        place = tile - 1 + side
        inside = jnp.logical_and(place >= 0, place < n_tile - 1)
        place = jnp.clip(place, 0, n_tile - 2)
        section = jnp.clip(section, 0, 2 * n_sec - 1)
        return jnp.where(inside, seam[place, section], 0).astype(F32)

    w3m[...] = w3[...]
    for kx in range(3):
        rows = slice(kx * CH, (kx + 1) * CH)
        w2m[rows, :] = jnp.concatenate([w2[ky, kx].astype(F32) for ky in range(3)], axis=1).astype(BF16)
        d2m[rows, :] = jnp.concatenate([d2[ky, kx].astype(F32) for ky in range(3)], axis=1).astype(BF16)
        d1m[rows, :] = jnp.concatenate(
            [d1[ky, kx].astype(F32)[:, 0:EVEN] for ky in range(3)]
            + [d1[ky, kx].astype(F32)[:, EVEN:DISP] for ky in range(3)]
            + [jnp.zeros((CH, K1 - 3 * DISP), F32)],
            axis=1,
        ).astype(BF16)
    d3m[...] = jnp.zeros_like(d3m)
    for kx in range(3):
        d3m[kx * 8 : kx * 8 + 2, :] = jnp.concatenate([d3[ky, kx].astype(F32) for ky in range(3)], axis=1)
    raw[...] = jnp.zeros_like(raw)
    for n in range(6):
        for y in [*range(1, ROWS + 1), *range(ROWS + 2, ROWS + 7)]:
            cost[n, y * PAD + EVEN : (y + 1) * PAD, :] = jnp.zeros((8, COLS), F32)

    pl.semaphore_wait(barrier, len(peers))

    def img_copy(k, dt, i):
        dst = own_img if k == 0 else far_img.at[int(k < 0)]
        src, rows = {-1: (img.at[:, 0:16], slice(48, 64)), 0: (img, slice(16, 48)), 1: (img.at[:, 16:32], slice(0, 16))}[dt]
        return pltpu.make_async_remote_copy(
            src_ref=src, dst_ref=dst.at[:, rows], send_sem=img_send.at[i], recv_sem=img_recv.at[i],
            device_id=at(k, dt), device_id_type=MESH,
        )

    img_copies = [img_copy(k, dt, i) for i, (k, dt) in enumerate([p for p in peers if p[0] in (0, -2, 2)])]
    for copy in img_copies:
        copy.start()

    for copy in img_copies[:2]:
        copy.wait_recv()

    base = 2 * sec

    def encode(below, mid, above, lower, upper, rim, write):
        below = dot(below, pick[...]) * lower
        mid = dot(mid, pick[...])
        above = dot(above, pick[...]) * upper
        for kx in range(3):
            cols = slice(kx * COLS, (kx + 1) * COLS)
            taps[pl.ds(kx, 16, stride=3), :] = below[:, cols]
            taps[pl.ds(48 + kx, 32, stride=3), :] = mid[:, cols]
            taps[pl.ds(144 + kx, 16, stride=3), :] = above[:, cols]

        for y in range(-rim - 2, ROWS + rim + 2, 2):
            at_row = 6 * y + 45
            x = jnp.concatenate([taps[at_row : at_row + 16, :], taps[at_row + 6 : at_row + 22, :]], axis=1)
            v = leaky(dot(w1m[...], x.astype(BF16)))
            if y >= ROWS:
                v = v * upper
            v = v.astype(BF16)
            for h in range(2):
                vh = v[:, h * COLS : (h + 1) * COLS]
                for ky in range(3):
                    to = y + h + 2 - 2 * ky
                    if -rim <= to < ROWS + rim:
                        first3[to + RADIUS, ky * CH : (ky + 1) * CH, :] = vh

        for y in range(-rim, ROWS + rim, 2):
            x = jnp.concatenate([first3[y + RADIUS], first3[y + RADIUS + 1]], axis=1)
            o = dot(w2m[...], x)
            for h in range(2):
                second[y + h + RADIUS] = leaky(fold(o, h, 2, CH)).astype(BF16)

        for y in range(-rim, ROWS + rim, 2):
            z = jnp.concatenate([second[y + RADIUS], second[y + RADIUS + 1]], axis=1)
            d = dot(w3m[...], z).astype(BF16)
            for h in range(2):
                write(y + h, d[:, h * COLS : (h + 1) * COLS])

    RIMS = {
        -1: (slice(RADIUS, 2 * RADIUS), slice(RADIUS + ROWS, EXT)),
        0: (slice(RADIUS, RADIUS + ROWS), slice(RADIUS, RADIUS + ROWS)),
        1: (slice(ROWS, RADIUS + ROWS), slice(0, RADIUS)),
    }

    def near_copy(s, k, dt, i):
        src, dst = RIMS[dt]
        return pltpu.make_async_remote_copy(
            src_ref=held.at[2 + s, src], dst_ref=held.at[2 + s - 2 * k, dst],
            send_sem=near_send.at[s, i], recv_sem=near_recv.at[s, i],
            device_id=at(k, dt), device_id_type=MESH,
        )

    def near_copies(s, batch):
        if batch == 0:
            k = 2 * s - 1
            return [near_copy(s, k, dt, dt + 1) for dt in (0, -1, 1)] + [near_copy(s, 0, -1, 3), near_copy(s, 0, 1, 4)]
        return [near_copy(s, 1 - 2 * s, dt, dt + 6) for dt in (0, -1, 1)]

    def encode_own(s, carry):
        def write(y, d):
            held[2 + s, RADIUS + y] = d
            desc_cy[s, pl.ds(y, DESC, stride=ROWS), :] = d.astype(F32)

        encode(own_img[s, 0:16], img[s], own_img[s, 48:64], link(base + s, 0), link(base + s, 1), 0, write)
        for copy in near_copies(s, 0):
            copy.start()
        return carry

    lax.fori_loop(0, 2, encode_own, 0)

    def near_rest(s, carry):
        for copy in near_copies(s, 1):
            copy.start()
        return carry

    lax.fori_loop(0, 2, near_rest, 0)

    def partner_links(s, j):
        ahead, behind = base + s + OFFSETS[j], base + s - OFFSETS[j]
        flag = partners[s, j] == ahead
        return flag, jnp.where(flag, link(ahead, 0), link(behind, 0)), jnp.where(flag, link(ahead, 1), link(behind, 1))

    lane = lax.broadcasted_iota(jnp.int32, (COLS, COLS), 1)

    def spread(i, carry):
        s, chunk = i // 4, lax.rem(i, 4)
        rows = pl.ds(pl.multiple_of(chunk * COLS, COLS), COLS)
        own = desc_cy[s, rows, :]
        desc_out[s, pl.ds(chunk * 8, 8)] = own.reshape(8, ROWS, COLS).astype(BF16)
        scaled = own * (1.0 / math.sqrt(DESC))
        for b in range(SPAN):
            d = b - RADIUS
            moved = pltpu.roll(scaled, d % COLS, 1) if d else scaled
            keep = jnp.logical_and(lane - d >= 0, lane - d < COLS)
            own_rot[s, b, rows, :] = jnp.where(keep, moved, 0.0)
        return carry

    lax.fori_loop(0, 8, spread, 0, unroll=2)

    for copy in img_copies[2:]:
        copy.wait_recv()

    def encode_far(s, carry):
        flag, lower, upper = partner_links(s, 2)

        def write(y, d):
            d = d.astype(F32)
            if y < 0:
                d = d * lower
            elif y >= ROWS:
                d = d * upper
            part[4 + s, pl.ds(y + RADIUS, DESC, stride=EXT), :] = d

        chosen = jnp.where(flag, far_img[1, s].astype(F32), far_img[0, s].astype(F32)).astype(BF16)
        encode(chosen[0:16], chosen[16:48], chosen[48:64], lower, upper, RADIUS, write)
        return carry

    lax.fori_loop(0, 2, encode_far, 0)

    def edge_copy(stage, n, direction):
        if stage == 0:
            at_src, at_dst = ((1, ROWS + 1), (ROWS, 0))[direction]
            src = cost.at[n, at_src * PAD : (at_src + 1) * PAD]
            dst = cost.at[n, at_dst * PAD : (at_dst + 1) * PAD]
        else:
            buf = (hid1, hid2)[stage - 1]
            if direction == 0:
                src, dst = buf.at[n, 1, CH : 2 * CH], buf.at[n, ROWS, 2 * CH : 3 * CH]
            else:
                src, dst = buf.at[n, ROWS, CH : 2 * CH], buf.at[n, 1, 0:CH]
        return pltpu.make_async_remote_copy(
            src_ref=src, dst_ref=dst,
            send_sem=edge_send.at[stage, n, direction], recv_sem=edge_recv.at[stage, n, direction],
            device_id=at(0, 2 * direction - 1), device_id_type=MESH,
        )

    def gather(j, s):
        flag, lower, upper = partner_links(s, j)

        def row(y, carry):
            ahead = held[2 + s + OFFSETS[j], y].astype(F32)
            behind = held[2 + s - OFFSETS[j], y].astype(F32)
            m = jnp.where(y < RADIUS, lower, jnp.where(y >= RADIUS + ROWS, upper, 1.0))
            part[2 * j + s, pl.ds(y, DESC, stride=EXT), :] = jnp.where(flag, ahead, behind) * m
            return carry

        lax.fori_loop(0, EXT, row, 0, unroll=12)

    def near_parts(j):
        for s in range(2):
            for copy in near_copies(s, j):
                copy.wait_recv()
        lax.fori_loop(0, 2, lambda s, carry: (gather(j, s), carry)[1], 0)

    def correlate(i, carry):
        n = lax.rem(i + 4, 6)
        s = lax.rem(n, 2)
        pl.when(i == 2)(lambda: near_parts(0))
        pl.when(i == 4)(lambda: near_parts(1))

        def place(b):
            for a in range(SPAN):
                moved = pltpu.roll(raw[a], lax.rem(COLS + RADIUS - b, COLS), 1)
                cost[n, pl.ds(PAD + a * SPAN + b, ROWS, stride=PAD), :] = moved

        def column(b, carry):
            place(jnp.maximum(b - 1, 0))
            acc = [None] * SPAN
            for c in range(DESC):
                own = own_rot[s, b, c * ROWS : (c + 1) * ROWS, :]
                for a in range(SPAN):
                    term = own * part[n, c * EXT + a : c * EXT + a + ROWS, :]
                    acc[a] = term if c == 0 else acc[a] + term
            for a in range(SPAN):
                raw[a] = acc[a]
            return carry

        lax.fori_loop(0, SPAN, column, 0, unroll=9)
        place(SPAN - 1)
        for direction in (0, 1):
            edge_copy(0, n, direction).start()
        return carry

    def hidden_rows(n, q, o, buf):
        for h in range(2):
            v = leaky(fold(o, h, 1, CH)).astype(BF16)
            for ky in range(3):
                buf[n, 2 * q + h + 2 - ky, ky * CH : (ky + 1) * CH, :] = v

    def decode_one(i, carry):
        n = lax.rem(i + 4, 6)
        s = lax.rem(n, 2)
        for direction in (0, 1):
            edge_copy(0, n, direction).wait_recv()
        cost[n, 0:PAD, :] = cost[n, 0:PAD, :] * link(base + s, 0)
        top = slice((ROWS + 1) * PAD, (ROWS + 2) * PAD)
        cost[n, top, :] = cost[n, top, :] * link(base + s, 1)

        def rows(q, carry):
            taps_of = []
            for h in range(2):
                start = pl.multiple_of((2 * q + h) * PAD, 8)
                taps_of.append(jnp.concatenate(
                    [cost[n, pl.ds(start + ky * PAD, EVEN), :] for ky in range(3)]
                    + [cost[n, pl.ds(start + EVEN, 8, stride=PAD), :]],
                    axis=0,
                ))
            x = jnp.concatenate(taps_of, axis=1)
            hidden_rows(n, q, dot(d1m[...], x.astype(BF16)), hid1)
            return carry

        lax.fori_loop(0, ROWS // 2, rows, 0, unroll=8)
        for direction in (0, 1):
            edge_copy(1, n, direction).start()
        return carry


    def rims(stage, n, buf):
        s = lax.rem(n, 2)
        for direction in (0, 1):
            edge_copy(stage, n, direction).wait_recv()
        buf[n, 1, 0:CH, :] = (buf[n, 1, 0:CH, :].astype(F32) * link(base + s, 0)).astype(BF16)
        top = slice(2 * CH, 3 * CH)
        buf[n, ROWS, top, :] = (buf[n, ROWS, top, :].astype(F32) * link(base + s, 1)).astype(BF16)

    def decode_two(i, carry):
        n = lax.rem(i + 4, 6)
        rims(1, n, hid1)

        def rows(q, carry):
            x = jnp.concatenate([hid1[n, 2 * q + 1], hid1[n, 2 * q + 2]], axis=1)
            hidden_rows(n, q, dot(d2m[...], x), hid2)
            return carry

        lax.fori_loop(0, ROWS // 2, rows, 0, unroll=8)
        for direction in (0, 1):
            edge_copy(2, n, direction).start()
        return carry


    def decode_three(i, carry):
        n = lax.rem(i + 4, 6)
        rims(2, n, hid2)
        weights = d3m[...].astype(BF16)

        def rows(q, carry):
            x = jnp.concatenate([hid2[n, 2 * q + 1], hid2[n, 2 * q + 2]], axis=1)
            o = dot(weights, x)
            for h in range(2):
                flow_y[pl.ds(pl.multiple_of((2 * q + h) * 8, 8), 8), :] = fold(o, h, 1, 8)
            return carry

        lax.fori_loop(0, ROWS // 2, rows, 0, unroll=8)
        s, j = lax.rem(n, 2), n // 2
        for o in range(2):
            flow_out[s, j, o] = flow_y[pl.ds(o, ROWS, stride=8), :]
        return carry


    lax.fori_loop(0, 6, correlate, 0)
    lax.fori_loop(0, 6, decode_one, 0)
    lax.fori_loop(0, 6, decode_two, 0)
    lax.fori_loop(0, 6, decode_three, 0)

    for copy in img_copies:
        copy.wait_send()

    def near_drain(s, carry):
        for copy in near_copies(s, 0) + near_copies(s, 1):
            copy.wait_send()
        return carry

    lax.fori_loop(0, 2, near_drain, 0)

    def drain(n, carry):
        for stage in range(3):
            for direction in (0, 1):
                edge_copy(stage, n, direction).wait_send()
        return carry

    lax.fori_loop(0, 6, drain, 0)


def solution(mesh):
    n_sec, n_tile = mesh.shape["sec"], mesh.shape["tile"]
    vmem = pl.BlockSpec(memory_space=pltpu.VMEM)
    smem = pl.BlockSpec(memory_space=pltpu.SMEM)
    dma = pltpu.SemaphoreType.DMA

    def shards(images, seam_links, partners, enc_first, enc_second, enc_third, dec_first, dec_second, dec_third):
        taps_first = lambda w: jnp.transpose(w, (2, 3, 0, 1))
        return pl.pallas_call(
            functools.partial(kernel, n_sec, n_tile),
            out_shape=(
                jax.ShapeDtypeStruct((2, DESC, ROWS, COLS), BF16),
                jax.ShapeDtypeStruct((2, 3, 2, ROWS, COLS), F32),
            ),
            in_specs=[smem, smem] + [vmem] * 7,
            out_specs=(vmem, vmem),
            scratch_shapes=[
                pltpu.VMEM((2, 64, 256), BF16),
                pltpu.VMEM((2, 2, 64, 256), BF16),
                pltpu.VMEM((192, COLS), F32),
                pltpu.VMEM((256, 3 * COLS), BF16),
                pltpu.VMEM((CH, 16), BF16),
                pltpu.VMEM((3 * CH, 3 * CH), BF16),
                pltpu.VMEM((DESC, CH), BF16),
                pltpu.VMEM((3 * CH, K1), BF16),
                pltpu.VMEM((3 * CH, 3 * CH), BF16),
                pltpu.VMEM((24, 3 * CH), F32),
                pltpu.VMEM((EXT, 3 * CH, COLS), BF16),
                pltpu.VMEM((EXT, CH, COLS), BF16),
                pltpu.VMEM((2, DESC * ROWS, COLS), F32),
                pltpu.VMEM((2, SPAN, DESC * ROWS, COLS), F32),
                pltpu.VMEM((6, EXT, DESC, COLS), BF16),
                pltpu.VMEM((6, DESC * EXT, COLS), F32),
                pltpu.VMEM((SPAN, ROWS, COLS), F32),
                pltpu.VMEM((6, (ROWS + 7) * PAD, COLS), F32),
                pltpu.VMEM((6, ROWS + 2, 3 * CH, COLS), BF16),
                pltpu.VMEM((6, ROWS + 2, 3 * CH, COLS), BF16),
                pltpu.VMEM((ROWS * 8, COLS), F32),
                dma((8,)), dma((8,)), dma((2, 9)), dma((2, 9)),
                dma((3, 6, 2)), dma((3, 6, 2)),
            ],
            compiler_params=pltpu.CompilerParams(
                collective_id=0, has_side_effects=True, vmem_limit_bytes=56 * 1024 * 1024
            ),
        )(
            jnp.transpose(seam_links), partners, images,
            jnp.transpose(enc_first, (1, 2, 3, 0))[0], taps_first(enc_second), taps_first(enc_third)[0, 0],
            taps_first(dec_first), taps_first(dec_second), taps_first(dec_third),
        )

    return jax.shard_map(
        shards,
        mesh=mesh,
        in_specs=(P("sec", "tile", None), P(), P("sec", None), P(), P(), P(), P(), P(), P()),
        out_specs=(P("sec", None, "tile", None), P("sec", None, None, "tile", None)),
        check_vma=False,
    )
```
